32 devices in a mesh: gy: 8 (over z, y), gz: 4 (over x, core).
Axes of the slice: x: 2, y: 2, z: 4, core: 2. Of those that a mesh axis runs over, the one named last changes fastest.
Arguments:
- image: float32 [16, 128, 2048], P(None, 'gy', 'gz'), may hold values from -6 to 6
- seeds: int32 [16, 128, 2048], P(None, 'gy', 'gz'), may hold values from 0 to 2, as said below
Outputs:
- potentials: float32 [2, 16, 128, 2048], P(None, None, 'gy', 'gz')
The draws below stay inside these ranges and needn't reach their ends.
Inputs may be any that keep to these rules, and one draw needn't show every extreme that they name: Every voxel is unlabeled, pore or grain; about a fifth of the voxels are seeds.
All inputs are finite; a program needn't handle non-finite values.
Results may differ from the reference program's by a relative error of at most 0.0001.
Values sent between devices are 32-bit elements; how exact they have to be, the bound alone decides.
No kernel may reach another device: no remote copies, remote signals or barrier semaphores. Data moves between devices by JAX's collectives and lax.ppermute only.
A program may use at most 64 MiB of HBM per device.

```python
import math
import jax
import jax.numpy as jnp
from jax import lax

NX = 16
ITERS = 4
NY = 128
NZ = 2048


def draw_seeds(key, part):
    key = jax.random.fold_in(key, 7)
    ticket = jax.random.randint(key, (NX, NY, NZ), 0, 10)
    return jnp.where(ticket == 8, 1, jnp.where(ticket == 9, 2, 0)).astype(jnp.int32)


def levels(key, shape, shards, smallest, largest):
    loudness = 1.0
    for dim, blocks in shards:
        steps = jax.random.uniform(jax.random.fold_in(jax.random.fold_in(key, 6), dim), (blocks,), jnp.float32, smallest / len(shards), largest / len(shards))
        loudness = loudness * jnp.repeat(jnp.exp(steps), shape[dim] // blocks).reshape((-1,) + (1,) * (len(shape) - 1 - dim))
    return loudness


def noise(rng, extent, spread, bound, split=(), kind=jnp.bfloat16):
    level = levels(rng, extent, split, -0.22, 0.18) if split else 1.0
    entries = jax.random.normal(rng, extent, jnp.float32) * spread * level
    return jnp.minimum(jnp.maximum(entries, -bound), bound).astype(kind)


def setup_inputs(seed: int = 0) -> dict:
    splits = jax.random.split(jax.random.key(seed), 3)
    return {
        "image": noise(splits[0], (NX, NY, NZ), 1.0, 6.0, ((1, 8), (2, 4)), jnp.float32),
        "seeds": draw_seeds(jax.random.fold_in(splits[2], 71), 0),
    }


edge_beta = 60.0
edge_floor = 0.05


def gauss_taps():
    raw = [math.exp(-0.5 * k * k) for k in range(-2, 3)]
    total = sum(raw)
    return [value / total for value in raw]


def smooth_along(field, axis):
    taps = gauss_taps()
    length = field.shape[axis]
    widths = [(0, 0)] * field.ndim
    widths[axis] = (2, 2)
    padded = jnp.pad(field, widths)
    result = jnp.zeros_like(field)
    for k in range(5):
        result = result + taps[k] * lax.slice_in_dim(padded, k, k + length, axis=axis)
    return result


def forward_weights(smoothed, axis):
    length = smoothed.shape[axis]
    step = lax.slice_in_dim(smoothed, 1, length, axis=axis) - lax.slice_in_dim(smoothed, 0, length - 1, axis=axis)
    weight = edge_floor + jnp.exp(-edge_beta * step * step)
    widths = [(0, 0)] * smoothed.ndim
    widths[axis] = (0, 1)
    return jnp.pad(weight, widths)


def backward_of(weight, axis):
    length = weight.shape[axis]
    widths = [(0, 0)] * weight.ndim
    widths[axis] = (1, 0)
    return lax.slice_in_dim(jnp.pad(weight, widths), 0, length, axis=axis)


def neighbours(fields, forward, backward):
    total = jnp.zeros_like(fields)
    for axis in range(3):
        widths = [(0, 0)] * 4
        widths[axis + 1] = (1, 1)
        padded = jnp.pad(fields, widths)
        length = fields.shape[axis + 1]
        upper = lax.slice_in_dim(padded, 2, length + 2, axis=axis + 1)
        lower = lax.slice_in_dim(padded, 0, length, axis=axis + 1)
        total = total + forward[axis] * upper + backward[axis] * lower
    return total


def inner(left, right):
    return jnp.sum(left * right, axis=(1, 2, 3))


def reference(image, seeds):
    smoothed = smooth_along(smooth_along(smooth_along(image, 0), 1), 2)
    forward = [forward_weights(smoothed, axis) for axis in range(3)]
    backward = [backward_of(forward[axis], axis) for axis in range(3)]
    degree = forward[0] + backward[0] + forward[1] + backward[1] + forward[2] + backward[2]
    free = (seeds == 0).astype(jnp.float32)
    marks = jnp.stack([(seeds == 1).astype(jnp.float32), (seeds == 2).astype(jnp.float32)])

    def operate(fields):
        return free * (degree * fields - neighbours(free * fields, forward, backward)) + (1.0 - free) * fields

    rhs = free * neighbours(marks, forward, backward)
    diag = free * degree + (1.0 - free)
    solution = jnp.zeros_like(rhs)
    resid = rhs
    precond = resid / diag
    direction = precond
    rz_now = inner(resid, precond)
    for step in range(ITERS):
        image_dir = operate(direction)
        alpha = (rz_now / inner(direction, image_dir))[:, None, None, None]
        solution = solution + alpha * direction
        resid = resid - alpha * image_dir
        precond = resid / diag
        rz_next = inner(resid, precond)
        direction = precond + (rz_next / rz_now)[:, None, None, None] * direction
        rz_now = rz_next
    return solution + marks
```

```python
import math

import jax
import jax.numpy as jnp
from jax import lax
from jax.experimental import pallas as pl
from jax.experimental.pallas import tpu as pltpu
from jax.sharding import PartitionSpec as P

ITERS = 4
FIELDS = 2
EDGE_BETA = 60.0
EDGE_FLOOR = 0.05
LANES = 128

IMG_BEFORE, IMG_AFTER = ITERS + 2, ITERS + 3
SEED_BEFORE, SEED_AFTER = ITERS, ITERS + 1
UP = IMG_BEFORE + SEED_BEFORE
DOWN = IMG_AFTER + SEED_AFTER
MOMENTS = 2 * ITERS


def gauss_taps():
    raw = [math.exp(-0.5 * k * k) for k in range(-2, 3)]
    total = sum(raw)
    return [value / total for value in raw]


def slab_of(ref, row, parity, rows, half):
    index = pl.ds(row + rows * parity, half, 2 * rows)
    return jnp.concatenate([ref[t, index, :] for t in range(ref.shape[0])], axis=1)


def tile_copies(source, staged, sems, inward=True):
    copies = []
    for t in range(staged.shape[0]):
        ends = (source.at[:, pl.ds(t * LANES, LANES)], staged.at[t])
        copies.append(pltpu.make_async_copy(*(ends if inward else ends[::-1]), sems.at[t]))
    return copies


def stage(pairs):
    copies = [copy for source, staged, sems in pairs for copy in tile_copies(source, staged, sems)]
    for copy in copies:
        copy.start()
    for copy in copies:
        copy.wait()


def pack_kernel(
    rows, half, image_hbm, seeds_hbm, up, down, right, left, image, seeds, image_sem, seeds_sem
):
    stage([(image_hbm, image, image_sem), (seeds_hbm, seeds, seeds_sem)])
    tiles = image.shape[0]
    for parity in range(2):
        for i in range(IMG_BEFORE):
            up[i, parity] = slab_of(image, rows - IMG_BEFORE + i, parity, rows, half)
        for i in range(SEED_BEFORE):
            up[IMG_BEFORE + i, parity] = slab_of(
                seeds, rows - SEED_BEFORE + i, parity, rows, half
            ).astype(jnp.float32)
        for i in range(IMG_AFTER):
            down[i, parity] = slab_of(image, i, parity, rows, half)
        for i in range(SEED_AFTER):
            down[IMG_AFTER + i, parity] = slab_of(seeds, i, parity, rows, half).astype(
                jnp.float32
            )
        lane = lax.broadcasted_iota(jnp.int32, (half, LANES), 1)
        for kind, source in enumerate((image, seeds)):
            head = jnp.zeros((half, LANES), jnp.float32)
            tail = jnp.zeros((half, LANES), jnp.float32)
            for row in range(rows):
                index = pl.ds(row + rows * parity, half, 2 * rows)
                first = source[0, index, :].astype(jnp.float32)
                last = source[tiles - 1, index, :].astype(jnp.float32)
                here = (lane >= 8 * row) & (lane < 8 * row + 8)
                shift = (8 * row) % LANES
                head = jnp.where(here, pltpu.roll(first, shift, 1) if shift else first, head)
                shift = (8 * row + 8) % LANES
                tail = jnp.where(here, pltpu.roll(last, shift, 1) if shift else last, tail)
            left[kind, parity] = head
            right[kind, parity] = tail


def main_kernel(
    rows,
    half,
    image_hbm,
    seeds_hbm,
    above,
    below,
    from_left,
    from_right,
    corner_above,
    corner_below,
    y_out,
    s_out,
    stats,
    x_ext,
    mark,
    smooth,
    scale,
    w_col,
    w_dep,
    w_row,
    w_raw,
    image,
    seeds,
    image_sem,
    seeds_sem,
):
    stage([(image_hbm, image, image_sem), (seeds_hbm, seeds, seeds_sem)])
    cols = image_hbm.shape[1]
    wide = cols + LANES
    gy, gz = lax.axis_index("gy"), lax.axis_index("gz")
    last_gy, last_gz = lax.axis_size("gy") - 1, lax.axis_size("gz") - 1
    t0, t1, t2 = gauss_taps()[:3]
    tile_lane = lax.broadcasted_iota(jnp.int32, (half, LANES), 1)

    def halo_tile(before, before_at, after, after_at):
        after_tile = pltpu.roll(after, (LANES - after_at) % LANES, 1) if after_at else after
        shift = (LANES - 8 - before_at) % LANES
        before_tile = pltpu.roll(before, shift, 1) if shift else before
        return jnp.where(
            tile_lane < 8, after_tile, jnp.where(tile_lane >= LANES - 8, before_tile, 0.0)
        )

    def put_image(index, parity, core, halo):
        x_ext[index, parity, :, 0:cols] = core
        x_ext[index, parity, :, cols:wide] = halo

    def put_seeds(index, parity, core, halo):
        for part, at in ((core, slice(0, cols)), (halo, slice(cols, wide))):
            mark[0, index, parity, :, at] = (part == 1.0).astype(jnp.float32)
            mark[1, index, parity, :, at] = (part == 2.0).astype(jnp.float32)

    def corner(ref, kind, parity, row):
        tile = ref[kind, parity]
        at = (8 * row) % 64
        return halo_tile(tile, 64 + at, tile, at)

    for parity in range(2):
        for i in range(IMG_BEFORE):
            put_image(
                i, parity, above[i, parity], corner(corner_above, 0, parity, rows - IMG_BEFORE + i)
            )
        for i in range(IMG_AFTER):
            put_image(
                IMG_BEFORE + rows + i, parity, below[i, parity], corner(corner_below, 0, parity, i)
            )
        for i in range(SEED_BEFORE):
            put_seeds(
                i,
                parity,
                above[IMG_BEFORE + i, parity],
                corner(corner_above, 1, parity, rows - SEED_BEFORE + i),
            )
        for i in range(SEED_AFTER):
            put_seeds(
                SEED_BEFORE + rows + i,
                parity,
                below[IMG_AFTER + i, parity],
                corner(corner_below, 1, parity, i),
            )
        for row in range(rows):
            put_image(
                IMG_BEFORE + row,
                parity,
                slab_of(image, row, parity, rows, half),
                halo_tile(from_left[0, parity], 8 * row, from_right[0, parity], 8 * row),
            )
            put_seeds(
                SEED_BEFORE + row,
                parity,
                slab_of(seeds, row, parity, rows, half).astype(jnp.float32),
                halo_tile(from_left[1, parity], 8 * row, from_right[1, parity], 8 * row),
            )

    sub = lax.broadcasted_iota(jnp.int32, (half, wide), 0)
    lane = lax.broadcasted_iota(jnp.int32, (half, wide), 1)
    not_first = (sub > 0).astype(jnp.float32)
    not_last = (sub < half - 1).astype(jnp.float32)

    def next_col(v):
        return pltpu.roll(v, wide - 1, 1)

    def prev_col(v):
        return pltpu.roll(v, 1, 1)

    def next_sub(v):
        return pltpu.roll(v, half - 1, 0)

    def prev_sub(v):
        return pltpu.roll(v, 1, 0)

    def smooth_row(r, carry):
        def along_rows(parity):
            return (
                t0 * (x_ext[r, parity] + x_ext[r + 4, parity])
                + t1 * (x_ext[r + 1, parity] + x_ext[r + 3, parity])
                + t2 * x_ext[r + 2, parity]
            )

        even, odd = along_rows(0), along_rows(1)
        even_up, even_dn = not_last * next_sub(even), not_first * prev_sub(even)
        odd_up, odd_dn = not_last * next_sub(odd), not_first * prev_sub(odd)
        deep = (
            t0 * (even_up + even_dn) + t1 * (odd + odd_dn) + t2 * even,
            t0 * (odd_up + odd_dn) + t1 * (even + even_up) + t2 * odd,
        )
        for parity in range(2):
            v = deep[parity]
            one = next_col(v) + prev_col(v)
            two = pltpu.roll(v, wide - 2, 1) + pltpu.roll(v, 2, 1)
            smooth[r, parity] = t0 * two + t1 * one + t2 * v
        return carry

    lax.fori_loop(0, rows + 2 * ITERS + 1, smooth_row, 0)

    cut_col = jnp.where(
        ((lane == wide - 1) & (gz == 0)) | ((lane == cols - 1) & (gz == last_gz)), 0.0, 1.0
    )

    def weight(step):
        return EDGE_FLOOR + jnp.exp((-EDGE_BETA * step) * step)

    def row_edge(i):
        cut = ((i == ITERS - 1) & (gy == 0)) | ((i == ITERS + rows - 1) & (gy == last_gy))
        keep = jnp.where(cut, 0.0, 1.0)
        for parity in range(2):
            w_raw[i, parity] = keep * weight(smooth[i + 1, parity] - smooth[i, parity])

    row_edge(0)
    zero_slab = jnp.zeros((half, wide), jnp.float32)
    scale[0, 0] = zero_slab
    scale[0, 1] = zero_slab

    def weigh_row(i, carry):
        row_edge(i)
        even, odd = smooth[i, 0], smooth[i, 1]
        dep = (weight(odd - even), not_last * weight(next_sub(even) - odd))
        col = [cut_col * weight(next_col(v) - v) for v in (even, odd)]
        dep_back = (prev_sub(dep[1]), dep[0])
        s = []
        for parity in range(2):
            deg = (
                dep[parity]
                + dep_back[parity]
                + w_raw[i, parity]
                + w_raw[i - 1, parity]
                + col[parity]
                + prev_col(col[parity])
            )
            free = 1.0 - mark[0, i, parity] - mark[1, i, parity]
            s.append(free * lax.rsqrt(deg))
        for f in range(FIELDS):
            m = (mark[f, i, 0], mark[f, i, 1])
            lower = (dep[0] * m[1] + prev_sub(dep[1] * m[1]), dep[1] * next_sub(m[0]) + dep[0] * m[0])
            for parity in range(2):
                total = (
                    lower[parity]
                    + col[parity] * next_col(m[parity])
                    + prev_col(col[parity] * m[parity])
                    + w_raw[i, parity] * mark[f, i + 1, parity]
                    + w_raw[i - 1, parity] * mark[f, i - 1, parity]
                )
                y_out[0, f, i, parity] = s[parity] * total
        w_dep[i, 0] = dep[0] * s[0] * s[1]
        w_dep[i, 1] = dep[1] * s[1] * next_sub(s[0])
        for parity in range(2):
            w_col[i, parity] = col[parity] * s[parity] * next_col(s[parity])
            w_row[i - 1, parity] = w_raw[i - 1, parity] * s[parity] * scale[i - 1, parity]
            scale[i, parity] = s[parity]
        return carry

    lax.fori_loop(1, rows + 2 * ITERS, weigh_row, 0)

    def fold(a, b):
        total = None
        for parity in range(2):
            for at in range(0, cols, LANES):
                part = a[parity][:, at : at + LANES] * b[parity][:, at : at + LANES]
                total = part if total is None else total + part
        return total

    def apply_row(level, f, i):
        even, odd = y_out[level - 1, f, i, 0], y_out[level - 1, f, i, 1]
        dep = (w_dep[i, 0], w_dep[i, 1])
        lower = (
            dep[0] * odd + prev_sub(dep[1] * odd),
            dep[1] * next_sub(even) + dep[0] * even,
        )
        fresh = []
        for parity, v in enumerate((even, odd)):
            col = w_col[i, parity]
            total = (
                lower[parity]
                + col * next_col(v)
                + prev_col(col * v)
                + w_row[i, parity] * y_out[level - 1, f, i + 1, parity]
                + w_row[i - 1, parity] * y_out[level - 1, f, i - 1, parity]
            )
            y_out[level, f, i, parity] = total
            fresh.append(total)
        return (even, odd), fresh

    zero = jnp.zeros((half, LANES), jnp.float32)
    sums = []
    for level in range(1, ITERS):

        def outer_row(i, carry, level=level):
            for f in range(FIELDS):
                apply_row(level, f, i)
            return carry

        def core_row(i, carry, level=level):
            carry = list(carry)
            out = []
            for f in range(FIELDS):
                old, new = apply_row(level, f, i)
                pairs = [(old, new), (new, new)]
                if level == 1:
                    pairs = [(old, old)] + pairs
                for a, b in pairs:
                    out.append(carry[len(out)] + fold(a, b))
            return tuple(out)

        count = 3 if level == 1 else 2
        lax.fori_loop(level + 1, ITERS, outer_row, 0)
        acc = lax.fori_loop(ITERS, ITERS + rows, core_row, (zero,) * (count * FIELDS))
        lax.fori_loop(ITERS + rows, rows + 2 * ITERS - level, outer_row, 0)
        sums.append([acc[:count], acc[count:]])

    def edge_row(i, carry):
        out = []
        for f in range(FIELDS):
            even, odd = y_out[ITERS - 1, f, i, 0], y_out[ITERS - 1, f, i, 1]
            forward = (
                w_dep[i, 0] * odd + w_col[i, 0] * next_col(even)
                + w_row[i, 0] * y_out[ITERS - 1, f, i + 1, 0],
                w_dep[i, 1] * next_sub(even) + w_col[i, 1] * next_col(odd)
                + w_row[i, 1] * y_out[ITERS - 1, f, i + 1, 1],
            )
            out.append(carry[f] + fold(forward, (even, odd)))
        return tuple(out)

    edge = lax.fori_loop(ITERS, ITERS + rows, edge_row, (zero,) * FIELDS)

    one_lane = lax.broadcasted_iota(jnp.int32, (1, LANES), 1)
    packed = jnp.zeros((1, LANES), jnp.float32)
    for f in range(FIELDS):
        parts = [p for level in sums for p in level[f]] + [2.0 * edge[f]]
        for k, part in enumerate(parts):
            value = jnp.sum(jnp.sum(part, axis=0, keepdims=True), axis=1, keepdims=True)
            packed = jnp.where(one_lane == f * MOMENTS + k, value, packed)
    stats[...] = packed
    s_out[...] = scale[ITERS : ITERS + rows, :, :, 0:cols]


def combine(a, b):
    out = [None] * (len(a) + len(b) - 1)
    for i, x in enumerate(a):
        for j, z in enumerate(b):
            out[i + j] = x * z if out[i + j] is None else out[i + j] + x * z
    return out


def weighted(coefs, values):
    total = coefs[0] * values[0]
    for c, v in zip(coefs[1:], values[1:]):
        total = total + c * v
    return total


def krylov_coefs(m):
    gaps = [m[k] - m[k + 1] for k in range(MOMENTS - 1)]
    one = jnp.ones_like(m[0])
    zero = jnp.zeros_like(m[0])
    resid, direct, result = [one], [one], [zero] * ITERS
    rz = m[0]
    for k in range(ITERS):
        curve = weighted(combine(direct, direct), gaps)
        alpha = rz / curve
        result = [
            result[i] + alpha * direct[i] if i < len(direct) else result[i] for i in range(ITERS)
        ]
        if k + 1 == ITERS:
            break
        image = [
            (direct[i] if i < len(direct) else zero) - (direct[i - 1] if i > 0 else zero)
            for i in range(len(direct) + 1)
        ]
        resid = [(resid[i] if i < len(resid) else zero) - alpha * image[i] for i in range(len(image))]
        rz_next = weighted(combine(resid, resid), m)
        ratio = rz_next / rz
        direct = [
            resid[i] + ratio * direct[i] if i < len(direct) else resid[i] for i in range(len(resid))
        ]
        rz = rz_next
    return result


def finish_kernel(rows, half, seeds_hbm, gathered, y, s, out_hbm, seeds, out, seeds_sem, out_sem):
    stage([(seeds_hbm, seeds, seeds_sem)])
    cols = seeds_hbm.shape[1]
    depth_rows = 2 * half * rows
    total = jnp.sum(gathered[...], axis=0, keepdims=True)
    one_lane = lax.broadcasted_iota(jnp.int32, (1, LANES), 1)
    coefs = []
    for f in range(FIELDS):
        moments = []
        for k in range(MOMENTS):
            pick = jnp.where(one_lane == f * MOMENTS + k, total, 0.0)
            value = jnp.sum(pick, axis=1, keepdims=True)
            moments.append(jnp.broadcast_to(value, (half, LANES)))
        coefs.append(krylov_coefs(moments))
    for f in range(FIELDS):
        for row in range(rows):
            for parity in range(2):
                label = slab_of(seeds, row, parity, rows, half)
                index = pl.ds(f * depth_rows + row + rows * parity, half, 2 * rows)
                for at in range(0, cols, LANES):
                    x = weighted(
                        coefs[f],
                        [y[k, f, ITERS + row, parity, :, at : at + LANES] for k in range(ITERS)],
                    )
                    x = x * s[row, parity, :, at : at + LANES]
                    hit = label[:, at : at + LANES] == f + 1
                    out[at // LANES, index, :] = x + hit.astype(jnp.float32)
    copies = tile_copies(out_hbm, out, out_sem, inward=False)
    for copy in copies:
        copy.start()
    for copy in copies:
        copy.wait()


def vmem(count):
    return [pl.BlockSpec(memory_space=pltpu.VMEM)] * count


def on_device(image, seeds):
    depth, rows, cols = image.shape
    half = depth // 2
    wide = cols + LANES
    f32 = jnp.float32
    flat_image = image.reshape(depth * rows, cols)
    flat_seeds = seeds.reshape(depth * rows, cols)
    params = pltpu.CompilerParams(vmem_limit_bytes=48 * 1024 * 1024)

    tiles = cols // LANES

    def call(kernel, shapes, raw, operands, scratch=(), raw_out=False):
        return pl.pallas_call(
            lambda *refs: kernel(rows, half, *refs),
            out_shape=[jax.ShapeDtypeStruct(shape, f32) for shape in shapes],
            in_specs=[pl.BlockSpec(memory_space=pl.ANY)] * len(raw) + vmem(len(operands)),
            out_specs=[pl.BlockSpec(memory_space=pl.ANY)] if raw_out else vmem(len(shapes)),
            scratch_shapes=list(scratch),
            compiler_params=params,
        )(*raw, *operands)

    def staged(dtype, height=depth * rows):
        return pltpu.VMEM((tiles, height, LANES), dtype)

    both = [staged(f32), staged(jnp.int32)] + [pltpu.SemaphoreType.DMA((tiles,))] * 2

    def forward(x, axis):
        return lax.ppermute(x, axis, [(i, i + 1) for i in range(lax.axis_size(axis) - 1)])

    def backward(x, axis):
        return lax.ppermute(x, axis, [(i + 1, i) for i in range(lax.axis_size(axis) - 1)])

    side = (2, 2, half, LANES)
    up, down, right, left = call(
        pack_kernel,
        [(UP, 2, half, cols), (DOWN, 2, half, cols), side, side],
        (flat_image, flat_seeds),
        (),
        both,
    )
    above = forward(up, "gy")
    below = backward(down, "gy")
    from_left = forward(right, "gz")
    from_right = backward(left, "gz")
    mid = LANES // 2
    corner_up = jnp.concatenate([from_right[..., mid:], from_left[..., mid:]], axis=-1)
    corner_down = jnp.concatenate([from_right[..., :mid], from_left[..., :mid]], axis=-1)
    corner_above = forward(corner_up, "gy")
    corner_below = backward(corner_down, "gy")

    span = rows + 2 * ITERS + 1
    slab = (span, 2, half, wide)
    y, s, stats = call(
        main_kernel,
        [(ITERS, FIELDS) + slab, (rows, 2, half, cols), (1, LANES)],
        (flat_image, flat_seeds),
        (above, below, from_left, from_right, corner_above, corner_below),
        [
            pltpu.VMEM(shape, f32)
            for shape in [(rows + IMG_BEFORE + IMG_AFTER, 2, half, wide), (FIELDS,) + slab] + [slab] * 6
        ]
        + both,
    )
    devices = lax.axis_size("gy") * lax.axis_size("gz")
    spread = jnp.broadcast_to(stats[None], (devices, 1, LANES))
    gathered = lax.all_to_all(spread, ("gy", "gz"), 0, 0).reshape(devices, LANES)
    (out,) = call(
        finish_kernel,
        [(FIELDS * depth * rows, cols)],
        (flat_seeds,),
        (gathered, y, s),
        [staged(jnp.int32), staged(f32, FIELDS * depth * rows)]
        + [pltpu.SemaphoreType.DMA((tiles,))] * 2,
        raw_out=True,
    )
    return out.reshape(FIELDS, depth, rows, cols)


def solution(mesh):
    return jax.shard_map(
        on_device,
        mesh=mesh,
        in_specs=(P(None, "gy", "gz"), P(None, "gy", "gz")),
        out_specs=P(None, None, "gy", "gz"),
        check_vma=False,
    )
```

```python
import math

import jax
import jax.numpy as jnp
from jax import lax
from jax.experimental import pallas as pl
from jax.experimental.pallas import tpu as pltpu
from jax.sharding import PartitionSpec as P

ITERS = 4
FIELDS = 2
EDGE_BETA = 60.0
EDGE_FLOOR = 0.05
LANES = 128

IMG_BEFORE, IMG_AFTER = ITERS + 2, ITERS + 3
SEED_BEFORE, SEED_AFTER = ITERS, ITERS + 1
UP = IMG_BEFORE + SEED_BEFORE
DOWN = IMG_AFTER + SEED_AFTER
MOMENTS = 2 * ITERS

SMOOTH_UNROLL = 5
WEIGH_UNROLL = 1
LEVEL_UNROLL = 4


def gauss_taps():
    raw = [math.exp(-0.5 * k * k) for k in range(-2, 3)]
    total = sum(raw)
    return [value / total for value in raw]


def slab_of(ref, row, parity, rows, half):
    index = pl.ds(row + rows * parity, half, 2 * rows)
    return jnp.concatenate([ref[t, index, :] for t in range(ref.shape[0])], axis=1)


def stage(pairs):
    copies = [
        pltpu.make_async_copy(source.at[:, pl.ds(t * LANES, LANES)], staged.at[t], sems.at[t])
        for source, staged, sems in pairs
        for t in range(staged.shape[0])
    ]
    for copy in copies:
        copy.start()
    for copy in copies:
        copy.wait()


def rows_kernel(rows, half, image_hbm, seeds_hbm, up, down, own, label, image, seeds, image_sem, seeds_sem):
    stage([(image_hbm, image, image_sem), (seeds_hbm, seeds, seeds_sem)])
    for row in range(rows):
        for parity in range(2):
            grey = slab_of(image, row, parity, rows, half)
            seed = slab_of(seeds, row, parity, rows, half).astype(jnp.float32)
            own[row, parity] = grey
            label[row, parity] = seed
            if row >= rows - IMG_BEFORE:
                up[row - (rows - IMG_BEFORE), parity] = grey
            if row >= rows - SEED_BEFORE:
                up[IMG_BEFORE + row - (rows - SEED_BEFORE), parity] = seed
            if row < IMG_AFTER:
                down[row, parity] = grey
            if row < SEED_AFTER:
                down[IMG_AFTER + row, parity] = seed


def cols_kernel(rows, half, own, label, right, left):
    cols = own.shape[3]
    lane = lax.broadcasted_iota(jnp.int32, (half, LANES), 1)
    for kind, source in enumerate((own, label)):
        for parity in range(2):
            head = jnp.zeros((half, LANES), jnp.float32)
            tail = jnp.zeros((half, LANES), jnp.float32)
            for row in range(rows):
                first = source[row, parity, :, 0:LANES]
                last = source[row, parity, :, cols - LANES : cols]
                here = (lane >= 8 * row) & (lane < 8 * row + 8)
                shift = (8 * row) % LANES
                head = jnp.where(here, pltpu.roll(first, shift, 1) if shift else first, head)
                shift = (8 * row + 8) % LANES
                tail = jnp.where(here, pltpu.roll(last, shift, 1) if shift else last, tail)
            left[kind, parity] = head
            right[kind, parity] = tail


def once(get):
    known = {}

    def value(parity, t):
        if (parity, t) not in known:
            known[parity, t] = get(parity, t)
        return known[parity, t]

    return value


def main_kernel(
    rows,
    half,
    own,
    label,
    above,
    below,
    from_left,
    from_right,
    corner_above,
    corner_below,
    basis,
    stats,
    x_ext,
    mark,
    smooth,
    scale,
    w_col,
    w_dep,
    w_row,
    w_raw,
    y,
):
    cols = own.shape[3]
    wide = cols + LANES
    tiles = wide // LANES
    core_tiles = cols // LANES
    gy, gz = lax.axis_index("gy"), lax.axis_index("gz")
    last_gy, last_gz = lax.axis_size("gy") - 1, lax.axis_size("gz") - 1
    t0, t1, t2 = gauss_taps()[:3]
    lane = lax.broadcasted_iota(jnp.int32, (half, LANES), 1)
    sub = lax.broadcasted_iota(jnp.int32, (half, LANES), 0)
    not_first = (sub > 0).astype(jnp.float32)
    not_last = (sub < half - 1).astype(jnp.float32)

    def at(t):
        return slice(t * LANES, (t + 1) * LANES)

    def halo_tile(before, before_at, after, after_at):
        after_tile = pltpu.roll(after, (LANES - after_at) % LANES, 1) if after_at else after
        shift = (LANES - 8 - before_at) % LANES
        before_tile = pltpu.roll(before, shift, 1) if shift else before
        return jnp.where(lane < 8, after_tile, jnp.where(lane >= LANES - 8, before_tile, 0.0))

    def put_image(index, parity, core, halo):
        for t in range(core_tiles):
            x_ext[index, parity, :, at(t)] = core[:, at(t)]
        x_ext[index, parity, :, at(core_tiles)] = halo

    def put_seeds(index, parity, core, halo):
        for t in range(tiles):
            part = core[:, at(t)] if t < core_tiles else halo
            for f in range(FIELDS):
                mark[f, index, parity, :, at(t)] = (part == f + 1.0).astype(jnp.float32)

    def corner(ref, kind, parity, row):
        tile = ref[kind, parity]
        place = (8 * row) % 64
        return halo_tile(tile, 64 + place, tile, place)

    for parity in range(2):
        for i in range(IMG_BEFORE):
            put_image(
                i, parity, above[i, parity], corner(corner_above, 0, parity, rows - IMG_BEFORE + i)
            )
        for i in range(IMG_AFTER):
            put_image(
                IMG_BEFORE + rows + i, parity, below[i, parity], corner(corner_below, 0, parity, i)
            )
        for i in range(SEED_BEFORE):
            put_seeds(
                i,
                parity,
                above[IMG_BEFORE + i, parity],
                corner(corner_above, 1, parity, rows - SEED_BEFORE + i),
            )
        for i in range(SEED_AFTER):
            put_seeds(
                SEED_BEFORE + rows + i,
                parity,
                below[IMG_AFTER + i, parity],
                corner(corner_below, 1, parity, i),
            )
        for row in range(rows):
            put_image(
                IMG_BEFORE + row,
                parity,
                own[row, parity],
                halo_tile(from_left[0, parity], 8 * row, from_right[0, parity], 8 * row),
            )
            put_seeds(
                SEED_BEFORE + row,
                parity,
                label[row, parity],
                halo_tile(from_left[1, parity], 8 * row, from_right[1, parity], 8 * row),
            )

    def shifted(get, by):
        turned = once(lambda parity, t: pltpu.roll(get(parity, t), -by % LANES, 1))
        if by > 0:
            return once(
                lambda parity, t: jnp.where(
                    lane < LANES - by, turned(parity, t), turned(parity, (t + 1) % tiles)
                )
            )
        return once(
            lambda parity, t: jnp.where(lane >= -by, turned(parity, t), turned(parity, (t - 1) % tiles))
        )

    def next_sub(v):
        return pltpu.roll(v, half - 1, 0)

    def prev_sub(v):
        return pltpu.roll(v, 1, 0)

    def load(ref, *index):
        return once(lambda parity, t: ref[(*index, parity, slice(None), at(t))])

    def every():
        return [(t, parity) for t in range(tiles) for parity in range(2)]

    def smooth_row(r, carry):
        x = [load(x_ext, r + k) for k in range(5)]
        flat = once(
            lambda p, t: t0 * (x[0](p, t) + x[4](p, t)) + t1 * (x[1](p, t) + x[3](p, t)) + t2 * x[2](p, t)
        )
        above_ = once(lambda p, t: not_last * next_sub(flat(p, t)))
        below_ = once(lambda p, t: not_first * prev_sub(flat(p, t)))

        def depth(p, t):
            if p == 0:
                near = flat(1, t) + below_(1, t)
            else:
                near = flat(0, t) + above_(0, t)
            return t0 * (above_(p, t) + below_(p, t)) + t1 * near + t2 * flat(p, t)

        deep = once(depth)
        near_next, near_prev = shifted(deep, 1), shifted(deep, -1)
        far_next, far_prev = shifted(deep, 2), shifted(deep, -2)
        for t, p in every():
            smooth[r, p, :, at(t)] = (
                t0 * (far_next(p, t) + far_prev(p, t))
                + t1 * (near_next(p, t) + near_prev(p, t))
                + t2 * deep(p, t)
            )
        return carry

    lax.fori_loop(0, rows + 2 * ITERS + 1, smooth_row, 0, unroll=SMOOTH_UNROLL)

    cut_tile = {
        core_tiles - 1: jnp.where((lane == LANES - 1) & (gz == last_gz), 0.0, 1.0),
        tiles - 1: jnp.where((lane == LANES - 1) & (gz == 0), 0.0, 1.0),
    }

    def weight(step):
        return EDGE_FLOOR + jnp.exp((-EDGE_BETA * step) * step)

    def row_edge(i, here):
        cut = ((i == ITERS - 1) & (gy == 0)) | ((i == ITERS + rows - 1) & (gy == last_gy))
        keep = jnp.where(cut, 0.0, 1.0)
        after = load(smooth, i + 1)
        return once(lambda p, t: keep * weight(after(p, t) - here(p, t)))

    first_edge = row_edge(0, load(smooth, 0))
    for t, p in every():
        w_raw[0, p, :, at(t)] = first_edge(p, t)
        scale[0, p, :, at(t)] = jnp.zeros((half, LANES), jnp.float32)

    def weigh_row(i, carry):
        here = load(smooth, i)
        down_edge, up_edge = row_edge(i, here), load(w_raw, i - 1)

        def dep_of(p, t):
            if p == 0:
                return weight(here(1, t) - here(0, t))
            return not_last * weight(next_sub(here(0, t)) - here(1, t))

        dep = once(dep_of)
        beyond = shifted(here, 1)

        def col_of(p, t):
            value = weight(beyond(p, t) - here(p, t))
            return cut_tile[t] * value if t in cut_tile else value

        col = once(col_of)
        col_back = shifted(col, -1)
        marks = [load(mark, f, i) for f in range(FIELDS)]

        def scale_of(p, t):
            back = prev_sub(dep(1, t)) if p == 0 else dep(0, t)
            deg = dep(p, t) + back + down_edge(p, t) + up_edge(p, t) + col(p, t) + col_back(p, t)
            return jnp.where(marks[0](p, t) + marks[1](p, t) == 0.0, lax.rsqrt(deg), 0.0)

        s = once(scale_of)
        s_beyond = shifted(s, 1)
        before = load(scale, i - 1)
        total = []
        for f in range(FIELDS):
            total.append(neighbour_sum(marks[f], dep, col, down_edge, up_edge, mark, f, i))
        for t, p in every():
            place = (p, slice(None), at(t))
            w_raw[(i, *place)] = down_edge(p, t)
            scale[(i, *place)] = s(p, t)
            w_row[(i - 1, *place)] = up_edge(p, t) * s(p, t) * before(p, t)
            other = s(1, t) if p == 0 else next_sub(s(0, t))
            w_dep[(i, *place)] = dep(p, t) * s(p, t) * other
            w_col[(i, *place)] = col(p, t) * s(p, t) * s_beyond(p, t)
            for f in range(FIELDS):
                y[(0, f, i, *place)] = s(p, t) * total[f](p, t)
        return carry

    def neighbour_sum(v, dep, col, down_edge, up_edge, ref, f, i):
        above_, below_ = load(ref, f, i - 1), load(ref, f, i + 1)
        beyond = shifted(v, 1)
        pushed = shifted(lambda p, t: col(p, t) * v(p, t), -1)

        def total(p, t):
            if p == 0:
                depth = dep(0, t) * v(1, t) + prev_sub(dep(1, t) * v(1, t))
            else:
                depth = dep(1, t) * next_sub(v(0, t)) + dep(0, t) * v(0, t)
            return (
                (depth + (col(p, t) * beyond(p, t) + pushed(p, t)))
                + (down_edge(p, t) * below_(p, t) + up_edge(p, t) * above_(p, t))
            )

        return once(total)

    lax.fori_loop(1, rows + 2 * ITERS, weigh_row, 0, unroll=WEIGH_UNROLL)

    zero = jnp.zeros((half, LANES), jnp.float32)
    inner = [(p, t) for t in range(core_tiles) for p in range(2)]

    def fold(a, b):
        total = None
        for p, t in inner:
            part = a(p, t) * b(p, t)
            total = part if total is None else total + part
        return total

    def weights_at(i):
        return load(w_dep, i), load(w_col, i), load(w_row, i), load(w_row, i - 1)

    def apply_row(level, i):
        weights = weights_at(i)
        olds = [load(y.at[level - 1], f, i) for f in range(FIELDS)]
        news = [
            neighbour_sum(olds[f], *weights, y.at[level - 1], f, i) for f in range(FIELDS)
        ]
        for t, p in every():
            for f in range(FIELDS):
                y[level, f, i, p, :, at(t)] = news[f](p, t)
        return olds, news

    def keep_basis(level, i, values):
        s = load(scale, i)
        for p, t in inner:
            for f in range(FIELDS):
                basis[level, f, i - ITERS, p, :, at(t)] = s(p, t) * values[f](p, t)

    sums = []
    for level in range(1, ITERS):

        def outer_row(i, carry, level=level):
            apply_row(level, i)
            return carry

        def core_row(i, carry, level=level):
            olds, news = apply_row(level, i)
            if level == 1:
                keep_basis(0, i, olds)
            keep_basis(level, i, news)
            out = []
            for f in range(FIELDS):
                pairs = [(olds[f], news[f]), (news[f], news[f])]
                if level == 1:
                    pairs = [(olds[f], olds[f])] + pairs
                for a, b in pairs:
                    out.append(carry[len(out)] + fold(a, b))
            return tuple(out)

        count = 3 if level == 1 else 2
        for i in (*range(level + 1, ITERS), *range(ITERS + rows, rows + 2 * ITERS - level)):
            outer_row(i, 0)
        acc = lax.fori_loop(
            ITERS, ITERS + rows, core_row, (zero,) * (count * FIELDS), unroll=LEVEL_UNROLL
        )
        sums.append([acc[:count], acc[count:]])

    def edge_row(i, carry):
        dep, col, row, _ = weights_at(i)
        out = []
        for f in range(FIELDS):
            v, below_ = load(y, ITERS - 1, f, i), load(y, ITERS - 1, f, i + 1)
            beyond = shifted(v, 1)

            def forward(p, t, v=v, below_=below_, beyond=beyond):
                lower = v(1, t) if p == 0 else next_sub(v(0, t))
                return dep(p, t) * lower + col(p, t) * beyond(p, t) + row(p, t) * below_(p, t)

            out.append(carry[f] + fold(once(forward), v))
        return tuple(out)

    edge = lax.fori_loop(ITERS, ITERS + rows, edge_row, (zero,) * FIELDS, unroll=LEVEL_UNROLL)

    one_lane = lax.broadcasted_iota(jnp.int32, (1, LANES), 1)
    packed = jnp.zeros((1, LANES), jnp.float32)
    for f in range(FIELDS):
        parts = [p for level in sums for p in level[f]] + [2.0 * edge[f]]
        for k, part in enumerate(parts):
            value = jnp.sum(jnp.sum(part, axis=0, keepdims=True), axis=1, keepdims=True)
            packed = jnp.where(one_lane == f * MOMENTS + k, value, packed)
    stats[...] = packed


def combine(a, b):
    out = [None] * (len(a) + len(b) - 1)
    for i, x in enumerate(a):
        for j, z in enumerate(b):
            out[i + j] = x * z if out[i + j] is None else out[i + j] + x * z
    return out


def weighted(coefs, values):
    total = coefs[0] * values[0]
    for c, v in zip(coefs[1:], values[1:]):
        total = total + c * v
    return total


def krylov_coefs(m):
    gaps = [m[k] - m[k + 1] for k in range(MOMENTS - 1)]
    one = jnp.ones_like(m[0])
    zero = jnp.zeros_like(m[0])
    resid, direct, result = [one], [one], [zero] * ITERS
    rz = m[0]
    for k in range(ITERS):
        curve = weighted(combine(direct, direct), gaps)
        alpha = jnp.where(curve > 0.0, rz / curve, 0.0)
        result = [
            result[i] + alpha * direct[i] if i < len(direct) else result[i] for i in range(ITERS)
        ]
        if k + 1 == ITERS:
            break
        image = [
            (direct[i] if i < len(direct) else zero) - (direct[i - 1] if i > 0 else zero)
            for i in range(len(direct) + 1)
        ]
        resid = [(resid[i] if i < len(resid) else zero) - alpha * image[i] for i in range(len(image))]
        rz_next = weighted(combine(resid, resid), m)
        ratio = jnp.where(rz > 0.0, rz_next / rz, 0.0)
        direct = [
            resid[i] + ratio * direct[i] if i < len(direct) else resid[i] for i in range(len(resid))
        ]
        rz = rz_next
    return result


def finish_kernel(rows, half, gathered, basis, label, out_hbm, out, out_sem):
    core_tiles = out.shape[1]
    total = jnp.sum(gathered[...], axis=0, keepdims=True)
    one_lane = lax.broadcasted_iota(jnp.int32, (1, LANES), 1)
    coefs = []
    for f in range(FIELDS):
        moments = []
        for k in range(MOMENTS):
            pick = jnp.where(one_lane == f * MOMENTS + k, total, 0.0)
            value = jnp.sum(pick, axis=1, keepdims=True)
            moments.append(jnp.broadcast_to(value, (half, LANES)))
        coefs.append(krylov_coefs(moments))
    depth_rows = 2 * half * rows
    copies = []
    for f in range(FIELDS):
        for t in range(core_tiles):
            at = slice(t * LANES, (t + 1) * LANES)
            for row in range(rows):
                for parity in range(2):
                    x = weighted(coefs[f], [basis[k, f, row, parity, :, at] for k in range(ITERS)])
                    hit = label[row, parity, :, at] == f + 1.0
                    index = pl.ds(row + rows * parity, half, 2 * rows)
                    out[f, t, index, :] = x + hit.astype(jnp.float32)
            copy = pltpu.make_async_copy(
                out.at[f, t],
                out_hbm.at[pl.ds(f * depth_rows, depth_rows), pl.ds(t * LANES, LANES)],
                out_sem.at[f, t],
            )
            copy.start()
            copies.append(copy)
    for copy in copies:
        copy.wait()


def vmem(count):
    return [pl.BlockSpec(memory_space=pltpu.VMEM)] * count


def hbm(count):
    return [pl.BlockSpec(memory_space=pltpu.HBM)] * count


def on_device(image, seeds):
    depth, rows, cols = image.shape
    half = depth // 2
    wide = cols + LANES
    core_tiles = cols // LANES
    f32 = jnp.float32

    def call(kernel, name, shapes, raw, operands, scratch=(), raw_out=False, mib=16):
        return pl.pallas_call(
            lambda *refs: kernel(rows, half, *refs),
            out_shape=[jax.ShapeDtypeStruct(shape, f32) for shape in shapes],
            in_specs=hbm(len(raw)) + vmem(len(operands)),
            out_specs=hbm(len(shapes)) if raw_out else vmem(len(shapes)),
            scratch_shapes=list(scratch),
            compiler_params=pltpu.CompilerParams(vmem_limit_bytes=mib * 1024 * 1024),
            name=name,
        )(*raw, *operands)

    def forward(x, axis):
        return lax.ppermute(x, axis, [(i, i + 1) for i in range(lax.axis_size(axis) - 1)])

    def backward(x, axis):
        return lax.ppermute(x, axis, [(i + 1, i) for i in range(lax.axis_size(axis) - 1)])

    def staged(dtype):
        return pltpu.VMEM((core_tiles, depth * rows, LANES), dtype)

    slabs = (rows, 2, half, cols)
    up, down, own, label = call(
        rows_kernel,
        "own_rows",
        [(UP,) + slabs[1:], (DOWN,) + slabs[1:], slabs, slabs],
        (image.reshape(depth * rows, cols), seeds.reshape(depth * rows, cols)),
        (),
        [staged(f32), staged(jnp.int32)] + [pltpu.SemaphoreType.DMA((core_tiles,))] * 2,
    )
    above = forward(up, "gy")
    below = backward(down, "gy")
    side = (2, 2, half, LANES)
    right, left = call(cols_kernel, "own_columns", [side, side], (), (own, label))
    from_left = forward(right, "gz")
    from_right = backward(left, "gz")
    mid = LANES // 2
    corner_up = jnp.concatenate([from_right[..., mid:], from_left[..., mid:]], axis=-1)
    corner_down = jnp.concatenate([from_right[..., :mid], from_left[..., :mid]], axis=-1)
    corner_above = forward(corner_up, "gy")
    corner_below = backward(corner_down, "gy")

    slab = (rows + 2 * ITERS + 1, 2, half, wide)
    shapes = [(rows + IMG_BEFORE + IMG_AFTER, 2, half, wide), (FIELDS,) + slab]
    shapes += [slab] * 6 + [(ITERS, FIELDS) + slab]
    basis, stats = call(
        main_kernel,
        "krylov",
        [(ITERS, FIELDS) + slabs, (1, LANES)],
        (),
        (own, label, above, below, from_left, from_right, corner_above, corner_below),
        [pltpu.VMEM(shape, f32) for shape in shapes],
        mib=32,
    )
    devices = lax.axis_size("gy") * lax.axis_size("gz")
    spread = jnp.broadcast_to(stats[None], (devices, 1, LANES))
    gathered = lax.all_to_all(spread, ("gy", "gz"), 0, 0).reshape(devices, LANES)
    (out,) = call(
        finish_kernel,
        "finish",
        [(FIELDS * depth * rows, cols)],
        (),
        (gathered, basis, label),
        [
            pltpu.VMEM((FIELDS, core_tiles, depth * rows, LANES), f32),
            pltpu.SemaphoreType.DMA((FIELDS, core_tiles)),
        ],
        raw_out=True,
    )
    return out.reshape(FIELDS, depth, rows, cols)


def solution(mesh):
    return jax.shard_map(
        on_device,
        mesh=mesh,
        in_specs=(P(None, "gy", "gz"), P(None, "gy", "gz")),
        out_specs=P(None, None, "gy", "gz"),
        check_vma=False,
    )
```

```python
import math

import jax
import jax.numpy as jnp
from jax import lax
from jax.experimental import pallas as pl
from jax.experimental.pallas import tpu as pltpu
from jax.sharding import PartitionSpec as P

ITERS = 4
FIELDS = 2
EDGE_BETA = 60.0
EDGE_FLOOR = 0.05
LANES = 128

IMG_BEFORE, IMG_AFTER = ITERS + 2, ITERS + 3
SEED_BEFORE, SEED_AFTER = ITERS, ITERS + 1
UP = IMG_BEFORE + SEED_BEFORE
DOWN = IMG_AFTER + SEED_AFTER
MOMENTS = 2 * ITERS

DEEP_UNROLL = 0
WIDE_UNROLL = 0
EDGE_UNROLL = 0
SCALE_UNROLL = 0
FIRST_UNROLL = 0
RESCALE_UNROLL = 0
LEVEL_UNROLL = 16


def gauss_taps():
    raw = [math.exp(-0.5 * k * k) for k in range(-2, 3)]
    total = sum(raw)
    return [value / total for value in raw]


def slab_of(ref, row, parity, rows, half):
    index = pl.ds(row + rows * parity, half, 2 * rows)
    return jnp.concatenate([ref[t, index, :] for t in range(ref.shape[0])], axis=1)


def stage(pairs):
    copies = [
        pltpu.make_async_copy(source.at[:, pl.ds(t * LANES, LANES)], staged.at[t], sems.at[t])
        for source, staged, sems in pairs
        for t in range(staged.shape[0])
    ]
    for copy in copies:
        copy.start()
    for copy in copies:
        copy.wait()


def rows_kernel(rows, half, image_hbm, seeds_hbm, up, down, own, label, image, seeds, image_sem, seeds_sem):
    stage([(image_hbm, image, image_sem), (seeds_hbm, seeds, seeds_sem)])
    for row in range(rows):
        for parity in range(2):
            grey = slab_of(image, row, parity, rows, half)
            seed = slab_of(seeds, row, parity, rows, half).astype(jnp.float32)
            own[row, parity] = grey
            label[row, parity] = seed
            if row >= rows - IMG_BEFORE:
                up[row - (rows - IMG_BEFORE), parity] = grey
            if row >= rows - SEED_BEFORE:
                up[IMG_BEFORE + row - (rows - SEED_BEFORE), parity] = seed
            if row < IMG_AFTER:
                down[row, parity] = grey
            if row < SEED_AFTER:
                down[IMG_AFTER + row, parity] = seed


def cols_kernel(rows, half, own, label, right, left):
    cols = own.shape[3]
    lane = lax.broadcasted_iota(jnp.int32, (half, LANES), 1)
    for kind, source in enumerate((own, label)):
        for parity in range(2):
            head = jnp.zeros((half, LANES), jnp.float32)
            tail = jnp.zeros((half, LANES), jnp.float32)
            for row in range(rows):
                first = source[row, parity, :, 0:LANES]
                last = source[row, parity, :, cols - LANES : cols]
                here = (lane >= 8 * row) & (lane < 8 * row + 8)
                shift = (8 * row) % LANES
                head = jnp.where(here, pltpu.roll(first, shift, 1) if shift else first, head)
                shift = (8 * row + 8) % LANES
                tail = jnp.where(here, pltpu.roll(last, shift, 1) if shift else last, tail)
            left[kind, parity] = head
            right[kind, parity] = tail


def once(get):
    known = {}

    def value(parity, t):
        if (parity, t) not in known:
            known[parity, t] = get(parity, t)
        return known[parity, t]

    return value


def main_kernel(
    rows,
    half,
    own,
    label,
    above,
    below,
    from_left,
    from_right,
    corner_above,
    corner_below,
    basis,
    stats,
    x_ext,
    mark,
    smooth,
    scale,
    w_col,
    w_dep,
    w_row,
    w_raw,
    y,
):
    cols = own.shape[3]
    wide = cols + LANES
    tiles = wide // LANES
    core_tiles = cols // LANES
    gy, gz = lax.axis_index("gy"), lax.axis_index("gz")
    last_gy, last_gz = lax.axis_size("gy") - 1, lax.axis_size("gz") - 1
    t0, t1, t2 = gauss_taps()[:3]
    lane = lax.broadcasted_iota(jnp.int32, (half, LANES), 1)
    sub = lax.broadcasted_iota(jnp.int32, (half, LANES), 0)
    not_first = (sub > 0).astype(jnp.float32)
    not_last = (sub < half - 1).astype(jnp.float32)

    def at(t):
        return slice(t * LANES, (t + 1) * LANES)

    def halo_tile(before, before_at, after, after_at):
        after_tile = pltpu.roll(after, (LANES - after_at) % LANES, 1) if after_at else after
        shift = (LANES - 8 - before_at) % LANES
        before_tile = pltpu.roll(before, shift, 1) if shift else before
        return jnp.where(lane < 8, after_tile, jnp.where(lane >= LANES - 8, before_tile, 0.0))

    def put_image(index, parity, core, halo):
        for t in range(core_tiles):
            x_ext[index, parity, :, at(t)] = core[:, at(t)]
        x_ext[index, parity, :, at(core_tiles)] = halo

    def put_seeds(index, parity, core, halo):
        for t in range(tiles):
            part = core[:, at(t)] if t < core_tiles else halo
            for f in range(FIELDS):
                mark[f, index, parity, :, at(t)] = (part == f + 1.0).astype(jnp.float32)

    def corner(ref, kind, parity, row):
        tile = ref[kind, parity]
        place = (8 * row) % 64
        return halo_tile(tile, 64 + place, tile, place)

    for parity in range(2):
        for i in range(IMG_BEFORE):
            put_image(
                i, parity, above[i, parity], corner(corner_above, 0, parity, rows - IMG_BEFORE + i)
            )
        for i in range(IMG_AFTER):
            put_image(
                IMG_BEFORE + rows + i, parity, below[i, parity], corner(corner_below, 0, parity, i)
            )
        for i in range(SEED_BEFORE):
            put_seeds(
                i,
                parity,
                above[IMG_BEFORE + i, parity],
                corner(corner_above, 1, parity, rows - SEED_BEFORE + i),
            )
        for i in range(SEED_AFTER):
            put_seeds(
                SEED_BEFORE + rows + i,
                parity,
                below[IMG_AFTER + i, parity],
                corner(corner_below, 1, parity, i),
            )
        for row in range(rows):
            put_image(
                IMG_BEFORE + row,
                parity,
                own[row, parity],
                halo_tile(from_left[0, parity], 8 * row, from_right[0, parity], 8 * row),
            )
            put_seeds(
                SEED_BEFORE + row,
                parity,
                label[row, parity],
                halo_tile(from_left[1, parity], 8 * row, from_right[1, parity], 8 * row),
            )

    def shifted(get, by):
        turned = once(lambda parity, t: pltpu.roll(get(parity, t), -by % LANES, 1))
        if by > 0:
            return once(
                lambda parity, t: jnp.where(
                    lane < LANES - by, turned(parity, t), turned(parity, (t + 1) % tiles)
                )
            )
        return once(
            lambda parity, t: jnp.where(lane >= -by, turned(parity, t), turned(parity, (t - 1) % tiles))
        )

    def next_sub(v):
        return pltpu.roll(v, half - 1, 0)

    def prev_sub(v):
        return pltpu.roll(v, 1, 0)

    def load(ref, *index):
        return once(lambda parity, t: ref[(*index, parity, slice(None), at(t))])

    def every():
        return [(t, parity) for t in range(tiles) for parity in range(2)]

    def deep_row(r):
        x = [load(x_ext, r + k) for k in range(5)]
        flat = once(
            lambda p, t: t0 * (x[0](p, t) + x[4](p, t)) + t1 * (x[1](p, t) + x[3](p, t)) + t2 * x[2](p, t)
        )
        above_ = once(lambda p, t: not_last * next_sub(flat(p, t)))
        below_ = once(lambda p, t: not_first * prev_sub(flat(p, t)))
        for t, p in every():
            near = flat(1, t) + below_(1, t) if p == 0 else flat(0, t) + above_(0, t)
            far = above_(p, t) + below_(p, t)
            smooth[r, p, :, at(t)] = t0 * far + t1 * near + t2 * flat(p, t)

    def wide_row(r):
        deep = load(smooth, r)
        near_next, near_prev = shifted(deep, 1), shifted(deep, -1)
        far_next, far_prev = shifted(deep, 2), shifted(deep, -2)
        fresh = {
            (p, t): t0 * (far_next(p, t) + far_prev(p, t))
            + t1 * (near_next(p, t) + near_prev(p, t))
            + t2 * deep(p, t)
            for t, p in every()
        }
        for (p, t), value in fresh.items():
            smooth[r, p, :, at(t)] = value

    cut_tile = {
        core_tiles - 1: jnp.where((lane == LANES - 1) & (gz == last_gz), 0.0, 1.0),
        tiles - 1: jnp.where((lane == LANES - 1) & (gz == 0), 0.0, 1.0),
    }

    def weight(step):
        return EDGE_FLOOR + jnp.exp((-EDGE_BETA * step) * step)

    def edges_row(i, cols_too=True):
        here, after = load(smooth, i), load(smooth, i + 1)
        cut = ((i == ITERS - 1) & (gy == 0)) | ((i == ITERS + rows - 1) & (gy == last_gy))
        keep = jnp.where(cut, 0.0, 1.0)
        beyond = shifted(here, 1)
        for t, p in every():
            place = (i, p, slice(None), at(t))
            w_raw[place] = keep * weight(after(p, t) - here(p, t))
            if cols_too:
                if p == 0:
                    w_dep[place] = weight(here(1, t) - here(0, t))
                else:
                    w_dep[place] = not_last * weight(next_sub(here(0, t)) - here(1, t))
                value = weight(beyond(p, t) - here(p, t))
                w_col[place] = cut_tile[t] * value if t in cut_tile else value

    def scale_row(i):
        dep, col, down_edge, up_edge = weights_at(i, w_raw)
        col_back = shifted(col, -1)
        marks = [load(mark, f, i) for f in range(FIELDS)]
        for t, p in every():
            back = prev_sub(dep(1, t)) if p == 0 else dep(0, t)
            deg = dep(p, t) + back + down_edge(p, t) + up_edge(p, t) + col(p, t) + col_back(p, t)
            free = marks[0](p, t) + marks[1](p, t) == 0.0
            scale[i, p, :, at(t)] = jnp.where(free, lax.rsqrt(deg), 0.0)

    def first_row(i):
        weights = weights_at(i, w_raw)
        s = load(scale, i)
        sums = [neighbour_sum(load(mark, f, i), *weights, mark, f, i) for f in range(FIELDS)]
        for t, p in every():
            for f in range(FIELDS):
                y[0, f, i, p, :, at(t)] = s(p, t) * sums[f](p, t)

    def rescale_row(i, cols_too=True):
        s, after = load(scale, i), load(scale, i + 1)
        dep, col, down_edge, _ = weights_at(i, w_raw)
        beyond = shifted(s, 1)
        for t, p in every():
            place = (i, p, slice(None), at(t))
            w_row[place] = down_edge(p, t) * s(p, t) * after(p, t)
            if cols_too:
                w_dep[place] = dep(p, t) * s(p, t) * (s(1, t) if p == 0 else next_sub(s(0, t)))
                w_col[place] = col(p, t) * s(p, t) * beyond(p, t)

    def weights_at(i, row_ref):
        return load(w_dep, i), load(w_col, i), load(row_ref, i), load(row_ref, i - 1)

    def run(body, first, stop, unroll):
        if unroll <= 0:
            for i in range(first, stop):
                body(i)
            return
        steps = (stop - first) // unroll

        def chunk(n, carry):
            for k in range(unroll):
                body(first + n * unroll + k)
            return carry

        lax.fori_loop(0, steps, chunk, 0)
        for i in range(first + steps * unroll, stop):
            body(i)

    def neighbour_sum(v, dep, col, down_edge, up_edge, ref, f, i):
        above_, below_ = load(ref, f, i - 1), load(ref, f, i + 1)
        beyond = shifted(v, 1)
        pushed = shifted(lambda p, t: col(p, t) * v(p, t), -1)

        def total(p, t):
            if p == 0:
                depth = dep(0, t) * v(1, t) + prev_sub(dep(1, t) * v(1, t))
            else:
                depth = dep(1, t) * next_sub(v(0, t)) + dep(0, t) * v(0, t)
            return (
                (depth + (col(p, t) * beyond(p, t) + pushed(p, t)))
                + (down_edge(p, t) * below_(p, t) + up_edge(p, t) * above_(p, t))
            )

        return once(total)

    last = rows + 2 * ITERS
    run(deep_row, 0, last + 1, DEEP_UNROLL)
    run(wide_row, 0, last + 1, WIDE_UNROLL)
    edges_row(0, False)
    run(edges_row, 1, last, EDGE_UNROLL)
    run(scale_row, 1, last, SCALE_UNROLL)
    run(first_row, 1, last, FIRST_UNROLL)
    rescale_row(1, False)
    run(rescale_row, 2, last - 1, RESCALE_UNROLL)

    zero = jnp.zeros((half, LANES), jnp.float32)
    inner = [(p, t) for t in range(core_tiles) for p in range(2)]

    def fold(a, b):
        total = None
        for p, t in inner:
            part = a(p, t) * b(p, t)
            total = part if total is None else total + part
        return total

    def apply_row(level, i):
        weights = weights_at(i, w_row)
        olds = [load(y.at[level - 1], f, i) for f in range(FIELDS)]
        news = [
            neighbour_sum(olds[f], *weights, y.at[level - 1], f, i) for f in range(FIELDS)
        ]
        for t, p in every():
            for f in range(FIELDS):
                y[level, f, i, p, :, at(t)] = news[f](p, t)
        return olds, news

    def keep_basis(level, i, values):
        s = load(scale, i)
        for p, t in inner:
            for f in range(FIELDS):
                basis[level, f, i - ITERS, p, :, at(t)] = s(p, t) * values[f](p, t)

    sums = []
    for level in range(1, ITERS):

        def outer_row(i, carry, level=level):
            apply_row(level, i)
            return carry

        def core_row(i, carry, level=level):
            olds, news = apply_row(level, i)
            if level == 1:
                keep_basis(0, i, olds)
            keep_basis(level, i, news)
            out = []
            for f in range(FIELDS):
                pairs = [(olds[f], news[f]), (news[f], news[f])]
                if level == 1:
                    pairs = [(olds[f], olds[f])] + pairs
                for a, b in pairs:
                    out.append(carry[len(out)] + fold(a, b))
            return tuple(out)

        count = 3 if level == 1 else 2
        for i in (*range(level + 1, ITERS), *range(ITERS + rows, rows + 2 * ITERS - level)):
            outer_row(i, 0)
        acc = lax.fori_loop(
            ITERS, ITERS + rows, core_row, (zero,) * (count * FIELDS), unroll=LEVEL_UNROLL
        )
        sums.append([acc[:count], acc[count:]])

    def edge_row(i, carry):
        dep, col, row, _ = weights_at(i, w_row)
        out = []
        for f in range(FIELDS):
            v, below_ = load(y, ITERS - 1, f, i), load(y, ITERS - 1, f, i + 1)
            beyond = shifted(v, 1)

            def forward(p, t, v=v, below_=below_, beyond=beyond):
                lower = v(1, t) if p == 0 else next_sub(v(0, t))
                return dep(p, t) * lower + col(p, t) * beyond(p, t) + row(p, t) * below_(p, t)

            out.append(carry[f] + fold(once(forward), v))
        return tuple(out)

    edge = lax.fori_loop(ITERS, ITERS + rows, edge_row, (zero,) * FIELDS, unroll=LEVEL_UNROLL)

    one_lane = lax.broadcasted_iota(jnp.int32, (1, LANES), 1)
    packed = jnp.zeros((1, LANES), jnp.float32)
    for f in range(FIELDS):
        parts = [p for level in sums for p in level[f]] + [2.0 * edge[f]]
        for k, part in enumerate(parts):
            value = jnp.sum(jnp.sum(part, axis=0, keepdims=True), axis=1, keepdims=True)
            packed = jnp.where(one_lane == f * MOMENTS + k, value, packed)
    stats[...] = packed


def combine(a, b):
    out = [None] * (len(a) + len(b) - 1)
    for i, x in enumerate(a):
        for j, z in enumerate(b):
            out[i + j] = x * z if out[i + j] is None else out[i + j] + x * z
    return out


def weighted(coefs, values):
    total = coefs[0] * values[0]
    for c, v in zip(coefs[1:], values[1:]):
        total = total + c * v
    return total


def krylov_coefs(m):
    gaps = [m[k] - m[k + 1] for k in range(MOMENTS - 1)]
    one = jnp.ones_like(m[0])
    zero = jnp.zeros_like(m[0])
    resid, direct, result = [one], [one], [zero] * ITERS
    rz = m[0]
    for k in range(ITERS):
        curve = weighted(combine(direct, direct), gaps)
        alpha = jnp.where(curve > 0.0, rz / curve, 0.0)
        result = [
            result[i] + alpha * direct[i] if i < len(direct) else result[i] for i in range(ITERS)
        ]
        if k + 1 == ITERS:
            break
        image = [
            (direct[i] if i < len(direct) else zero) - (direct[i - 1] if i > 0 else zero)
            for i in range(len(direct) + 1)
        ]
        resid = [(resid[i] if i < len(resid) else zero) - alpha * image[i] for i in range(len(image))]
        rz_next = weighted(combine(resid, resid), m)
        ratio = jnp.where(rz > 0.0, rz_next / rz, 0.0)
        direct = [
            resid[i] + ratio * direct[i] if i < len(direct) else resid[i] for i in range(len(resid))
        ]
        rz = rz_next
    return result


def finish_kernel(rows, half, gathered, basis, label, out_hbm, out, out_sem):
    core_tiles = out.shape[1]
    total = jnp.sum(gathered[...], axis=0, keepdims=True)
    one_lane = lax.broadcasted_iota(jnp.int32, (1, LANES), 1)
    coefs = []
    for f in range(FIELDS):
        moments = []
        for k in range(MOMENTS):
            pick = jnp.where(one_lane == f * MOMENTS + k, total, 0.0)
            value = jnp.sum(pick, axis=1, keepdims=True)
            moments.append(jnp.broadcast_to(value, (half, LANES)))
        coefs.append(krylov_coefs(moments))
    depth_rows = 2 * half * rows
    copies = []
    for f in range(FIELDS):
        for t in range(core_tiles):
            at = slice(t * LANES, (t + 1) * LANES)
            for row in range(rows):
                for parity in range(2):
                    x = weighted(coefs[f], [basis[k, f, row, parity, :, at] for k in range(ITERS)])
                    hit = label[row, parity, :, at] == f + 1.0
                    index = pl.ds(row + rows * parity, half, 2 * rows)
                    out[f, t, index, :] = x + hit.astype(jnp.float32)
            copy = pltpu.make_async_copy(
                out.at[f, t],
                out_hbm.at[pl.ds(f * depth_rows, depth_rows), pl.ds(t * LANES, LANES)],
                out_sem.at[f, t],
            )
            copy.start()
            copies.append(copy)
    for copy in copies:
        copy.wait()


def vmem(count):
    return [pl.BlockSpec(memory_space=pltpu.VMEM)] * count


def hbm(count):
    return [pl.BlockSpec(memory_space=pltpu.HBM)] * count


def on_device(image, seeds):
    depth, rows, cols = image.shape
    half = depth // 2
    wide = cols + LANES
    core_tiles = cols // LANES
    f32 = jnp.float32

    def call(kernel, name, shapes, raw, operands, scratch=(), raw_out=False, mib=16):
        return pl.pallas_call(
            lambda *refs: kernel(rows, half, *refs),
            out_shape=[jax.ShapeDtypeStruct(shape, f32) for shape in shapes],
            in_specs=hbm(len(raw)) + vmem(len(operands)),
            out_specs=hbm(len(shapes)) if raw_out else vmem(len(shapes)),
            scratch_shapes=list(scratch),
            compiler_params=pltpu.CompilerParams(vmem_limit_bytes=mib * 1024 * 1024),
            name=name,
        )(*raw, *operands)

    def forward(x, axis):
        return lax.ppermute(x, axis, [(i, i + 1) for i in range(lax.axis_size(axis) - 1)])

    def backward(x, axis):
        return lax.ppermute(x, axis, [(i + 1, i) for i in range(lax.axis_size(axis) - 1)])

    def staged(dtype):
        return pltpu.VMEM((core_tiles, depth * rows, LANES), dtype)

    slabs = (rows, 2, half, cols)
    up, down, own, label = call(
        rows_kernel,
        "own_rows",
        [(UP,) + slabs[1:], (DOWN,) + slabs[1:], slabs, slabs],
        tuple(
            pltpu.with_memory_space_constraint(v.reshape(depth * rows, cols), pltpu.HBM)
            for v in (image, seeds)
        ),
        (),
        [staged(f32), staged(jnp.int32)] + [pltpu.SemaphoreType.DMA((core_tiles,))] * 2,
    )
    above = forward(up, "gy")
    below = backward(down, "gy")
    side = (2, 2, half, LANES)
    right, left = call(cols_kernel, "own_columns", [side, side], (), (own, label))
    from_left = forward(right, "gz")
    from_right = backward(left, "gz")
    mid = LANES // 2
    corner_up = jnp.concatenate([from_right[..., mid:], from_left[..., mid:]], axis=-1)
    corner_down = jnp.concatenate([from_right[..., :mid], from_left[..., :mid]], axis=-1)
    corner_above = forward(corner_up, "gy")
    corner_below = backward(corner_down, "gy")

    slab = (rows + 2 * ITERS + 1, 2, half, wide)
    shapes = [(rows + IMG_BEFORE + IMG_AFTER, 2, half, wide), (FIELDS,) + slab]
    shapes += [slab] * 6 + [(ITERS, FIELDS) + slab]
    basis, stats = call(
        main_kernel,
        "krylov",
        [(ITERS, FIELDS) + slabs, (1, LANES)],
        (),
        (own, label, above, below, from_left, from_right, corner_above, corner_below),
        [pltpu.VMEM(shape, f32) for shape in shapes],
        mib=32,
    )
    devices = lax.axis_size("gy") * lax.axis_size("gz")
    spread = jnp.broadcast_to(stats[None], (devices, 1, LANES))
    gathered = lax.all_to_all(spread, ("gy", "gz"), 0, 0).reshape(devices, LANES)
    (out,) = call(
        finish_kernel,
        "finish",
        [(FIELDS * depth * rows, cols)],
        (),
        (gathered, basis, label),
        [
            pltpu.VMEM((FIELDS, core_tiles, depth * rows, LANES), f32),
            pltpu.SemaphoreType.DMA((FIELDS, core_tiles)),
        ],
        raw_out=True,
    )
    return out.reshape(FIELDS, depth, rows, cols)


def solution(mesh):
    return jax.shard_map(
        on_device,
        mesh=mesh,
        in_specs=(P(None, "gy", "gz"), P(None, "gy", "gz")),
        out_specs=P(None, None, "gy", "gz"),
        check_vma=False,
    )
```

```python
import math

import jax
import jax.numpy as jnp
from jax import lax
from jax.experimental import pallas as pl
from jax.experimental.pallas import tpu as pltpu
from jax.sharding import PartitionSpec as P

ITERS = 4
FIELDS = 2
EDGE_BETA = 60.0
EDGE_FLOOR = 0.05
LANES = 128

IMG_BEFORE, IMG_AFTER = ITERS + 2, ITERS + 3
SEED_BEFORE, SEED_AFTER = ITERS, ITERS + 1
UP = IMG_BEFORE + SEED_BEFORE
DOWN = IMG_AFTER + SEED_AFTER
MOMENTS = 2 * ITERS


def gauss_taps():
    raw = [math.exp(-0.5 * k * k) for k in range(-2, 3)]
    total = sum(raw)
    return [value / total for value in raw]


def slab_of(ref, row, parity, rows, half):
    index = pl.ds(row + rows * parity, half, 2 * rows)
    return jnp.concatenate([ref[t, index, :] for t in range(ref.shape[0])], axis=1)


def stage(pairs):
    copies = [
        pltpu.make_async_copy(source.at[:, pl.ds(t * LANES, LANES)], staged.at[t], sems.at[t])
        for source, staged, sems in pairs
        for t in range(staged.shape[0])
    ]
    for copy in copies:
        copy.start()
    for copy in copies:
        copy.wait()


def rows_kernel(rows, half, image_hbm, seeds_hbm, up, down, own, label, image, seeds, image_sem, seeds_sem):
    stage([(image_hbm, image, image_sem), (seeds_hbm, seeds, seeds_sem)])
    for row in range(rows):
        for parity in range(2):
            grey = slab_of(image, row, parity, rows, half)
            seed = slab_of(seeds, row, parity, rows, half).astype(jnp.float32)
            own[row, parity] = grey
            label[row, parity] = seed
            if row >= rows - IMG_BEFORE:
                up[row - (rows - IMG_BEFORE), parity] = grey
            if row >= rows - SEED_BEFORE:
                up[IMG_BEFORE + row - (rows - SEED_BEFORE), parity] = seed
            if row < IMG_AFTER:
                down[row, parity] = grey
            if row < SEED_AFTER:
                down[IMG_AFTER + row, parity] = seed


def cols_kernel(rows, half, own, label, pair, cross):
    even = lax.rem(lax.axis_index("gz"), 2) == 0
    cols = own.shape[3]
    lane = lax.broadcasted_iota(jnp.int32, (half, LANES), 1)
    for kind, source in enumerate((own, label)):
        for parity in range(2):
            head = jnp.zeros((half, LANES), jnp.float32)
            tail = jnp.zeros((half, LANES), jnp.float32)
            for row in range(rows):
                first = source[row, parity, :, 0:LANES]
                last = source[row, parity, :, cols - LANES : cols]
                here = (lane >= 8 * row) & (lane < 8 * row + 8)
                shift = (8 * row) % LANES
                head = jnp.where(here, pltpu.roll(first, shift, 1) if shift else first, head)
                shift = (8 * row + 8) % LANES
                tail = jnp.where(here, pltpu.roll(last, shift, 1) if shift else last, tail)
            pair[kind, parity] = jnp.where(even, tail, head)
            cross[kind, parity] = jnp.where(even, head, tail)


def once(get):
    known = {}

    def value(parity, t):
        if (parity, t) not in known:
            known[parity, t] = get(parity, t)
        return known[parity, t]

    return value


class Rows:
    def __init__(self, ref, first, lead=(), earlier=None):
        self.ref, self.first, self.lead, self.earlier = ref, first, lead, earlier

    def place(self, i, parity, t):
        lanes = slice(t * LANES, (t + 1) * LANES)
        return (*self.lead, i - self.first, parity, slice(None), lanes)

    def row(self, i):
        if self.earlier is not None and i < self.first:
            return self.earlier.row(i)
        return once(lambda parity, t: self.ref[self.place(i, parity, t)])

    def put(self, i, parity, t, value):
        self.ref[self.place(i, parity, t)] = value


WEIGHTS = ("smooth", "w_raw", "d_raw", "c_raw", "scale", "w_row", "w_dep", "w_col")


def extents(rows):
    table = {
        "image": (0, rows + IMG_BEFORE, rows + IMG_BEFORE + IMG_AFTER),
        "mark": (0, rows + SEED_BEFORE, rows + SEED_BEFORE + SEED_AFTER),
        "smooth": (0, rows + 2, rows + 2 * ITERS + 1),
        "w_raw": (0, rows + 1, rows + 2 * ITERS),
        "d_raw": (1, rows + 2, rows + 2 * ITERS),
        "c_raw": (1, rows + 2, rows + 2 * ITERS),
        "scale": (1, rows + 1, rows + 2 * ITERS),
        "w_row": (1, rows, rows + 2 * ITERS - 1),
        "w_dep": (2, rows + 1, rows + 2 * ITERS - 1),
        "w_col": (2, rows + 1, rows + 2 * ITERS - 1),
        "edge": (ITERS, rows + 1 - ITERS, rows + ITERS),
    }
    for level in range(ITERS):
        table["y", level] = (1 + level, rows + 1 - level, rows + 2 * ITERS - level)
    return table


def sweep(rows, half, second, fetch_image, fetch_seeds, stores, basis, basis_first, sums):
    span = {
        name: range(mid, stop) if second else range(first, mid)
        for name, (first, mid, stop) in extents(rows).items()
    }
    wide = stores["smooth"].ref.shape[-1]
    tiles = wide // LANES
    core_tiles = tiles - 1
    gy, gz = lax.axis_index("gy"), lax.axis_index("gz")
    last_gy, last_gz = lax.axis_size("gy") - 1, lax.axis_size("gz") - 1
    t0, t1, t2 = gauss_taps()[:3]
    lane = lax.broadcasted_iota(jnp.int32, (half, LANES), 1)
    sub = lax.broadcasted_iota(jnp.int32, (half, LANES), 0)
    not_first = (sub > 0).astype(jnp.float32)
    not_last = (sub < half - 1).astype(jnp.float32)
    every = [(t, p) for t in range(tiles) for p in range(2)]
    inner = [(t, p) for t in range(core_tiles) for p in range(2)]

    def shifted(get, by):
        turned = once(lambda parity, t: pltpu.roll(get(parity, t), -by % LANES, 1))
        if by > 0:
            return once(
                lambda parity, t: jnp.where(
                    lane < LANES - by, turned(parity, t), turned(parity, (t + 1) % tiles)
                )
            )
        return once(
            lambda parity, t: jnp.where(lane >= -by, turned(parity, t), turned(parity, (t - 1) % tiles))
        )

    def next_sub(v):
        return pltpu.roll(v, half - 1, 0)

    def prev_sub(v):
        return pltpu.roll(v, 1, 0)

    image, smooth, scale = stores["image"], stores["smooth"], stores["scale"]
    w_raw, d_raw, c_raw = stores["w_raw"], stores["d_raw"], stores["c_raw"]
    w_row, w_dep, w_col = stores["w_row"], stores["w_dep"], stores["w_col"]
    marks = [stores["mark", f] for f in range(FIELDS)]
    y = [[stores["y", level, f] for f in range(FIELDS)] for level in range(ITERS)]

    for i in span["image"]:
        for p in range(2):
            for t, part in enumerate(fetch_image(i, p, lane)):
                image.put(i, p, t, part)
    for i in span["mark"]:
        for p in range(2):
            for t, part in enumerate(fetch_seeds(i, p, lane)):
                for f in range(FIELDS):
                    marks[f].put(i, p, t, (part == f + 1.0).astype(jnp.float32))

    for i in span["smooth"]:
        x = [image.row(i + k) for k in range(5)]
        flat = once(
            lambda p, t, x=x: t0 * (x[0](p, t) + x[4](p, t))
            + t1 * (x[1](p, t) + x[3](p, t))
            + t2 * x[2](p, t)
        )
        later = once(lambda p, t, flat=flat: not_last * next_sub(flat(p, t)))
        sooner = once(lambda p, t, flat=flat: not_first * prev_sub(flat(p, t)))
        for t, p in every:
            near = flat(1, t) + sooner(1, t) if p == 0 else flat(0, t) + later(0, t)
            smooth.put(i, p, t, t0 * (later(p, t) + sooner(p, t)) + t1 * near + t2 * flat(p, t))
    for i in span["smooth"]:
        deep = smooth.row(i)
        near_next, near_prev = shifted(deep, 1), shifted(deep, -1)
        far_next, far_prev = shifted(deep, 2), shifted(deep, -2)
        fresh = [
            (
                p,
                t,
                t0 * (far_next(p, t) + far_prev(p, t))
                + t1 * (near_next(p, t) + near_prev(p, t))
                + t2 * deep(p, t),
            )
            for t, p in every
        ]
        for p, t, value in fresh:
            smooth.put(i, p, t, value)

    cut_tile = {
        core_tiles - 1: jnp.where((lane == LANES - 1) & (gz == last_gz), 0.0, 1.0),
        tiles - 1: jnp.where((lane == LANES - 1) & (gz == 0), 0.0, 1.0),
    }

    def weight(step):
        return EDGE_FLOOR + jnp.exp((-EDGE_BETA * step) * step)

    cut_row = {
        ITERS - 1: jnp.where(gy == 0, 0.0, 1.0),
        ITERS + rows - 1: jnp.where(gy == last_gy, 0.0, 1.0),
    }
    for i in sorted(set(span["w_raw"]) | set(span["d_raw"])):
        here = smooth.row(i)
        if i in span["w_raw"]:
            after = smooth.row(i + 1)
            for t, p in every:
                value = weight(after(p, t) - here(p, t))
                w_raw.put(i, p, t, cut_row[i] * value if i in cut_row else value)
        if i in span["d_raw"]:
            beyond = shifted(here, 1)
            for t, p in every:
                if p == 0:
                    d_raw.put(i, p, t, weight(here(1, t) - here(0, t)))
                else:
                    d_raw.put(i, p, t, not_last * weight(next_sub(here(0, t)) - here(1, t)))
                value = weight(beyond(p, t) - here(p, t))
                c_raw.put(i, p, t, cut_tile[t] * value if t in cut_tile else value)

    for i in span["scale"]:
        dep, col, down, up = d_raw.row(i), c_raw.row(i), w_raw.row(i), w_raw.row(i - 1)
        col_back = shifted(col, -1)
        seeded = [mark.row(i) for mark in marks]
        for t, p in every:
            back = prev_sub(dep(1, t)) if p == 0 else dep(0, t)
            deg = dep(p, t) + back + down(p, t) + up(p, t) + col(p, t) + col_back(p, t)
            free = seeded[0](p, t) + seeded[1](p, t) == 0.0
            scale.put(i, p, t, jnp.where(free, lax.rsqrt(deg), 0.0))

    def neighbour_sum(v, field, i, dep, col, down, up):
        above, below = field.row(i - 1), field.row(i + 1)
        beyond = shifted(v, 1)
        pushed = shifted(lambda p, t: col(p, t) * v(p, t), -1)

        def total(p, t):
            if p == 0:
                depth = dep(0, t) * v(1, t) + prev_sub(dep(1, t) * v(1, t))
            else:
                depth = dep(1, t) * next_sub(v(0, t)) + dep(0, t) * v(0, t)
            return (depth + (col(p, t) * beyond(p, t) + pushed(p, t))) + (
                down(p, t) * below(p, t) + up(p, t) * above(p, t)
            )

        return once(total)

    for i in span["y", 0]:
        edges = d_raw.row(i), c_raw.row(i), w_raw.row(i), w_raw.row(i - 1)
        s = scale.row(i)
        totals = [neighbour_sum(mark.row(i), mark, i, *edges) for mark in marks]
        for t, p in every:
            for f in range(FIELDS):
                y[0][f].put(i, p, t, s(p, t) * totals[f](p, t))

    for i in sorted(set(span["w_row"]) | set(span["w_dep"])):
        s = scale.row(i)
        if i in span["w_row"]:
            after, down = scale.row(i + 1), w_raw.row(i)
            for t, p in every:
                w_row.put(i, p, t, down(p, t) * s(p, t) * after(p, t))
        if i in span["w_dep"]:
            dep, col = d_raw.row(i), c_raw.row(i)
            beyond = shifted(s, 1)
            for t, p in every:
                other = s(1, t) if p == 0 else next_sub(s(0, t))
                w_dep.put(i, p, t, dep(p, t) * s(p, t) * other)
                w_col.put(i, p, t, col(p, t) * s(p, t) * beyond(p, t))

    sums = [list(column) for column in sums]

    def add_products(f, k, a, b):
        total = None
        for t, p in inner:
            part = a(p, t) * b(p, t)
            total = part if total is None else total + part
        sums[f][k] = total if sums[f][k] is None else sums[f][k] + total

    def keep_basis(level, i, values):
        s = scale.row(i)
        for t, p in inner:
            for f in range(FIELDS):
                lanes = slice(t * LANES, (t + 1) * LANES)
                basis[level, f, i - ITERS - basis_first, p, :, lanes] = s(p, t) * values[f](p, t)

    own = range(ITERS, ITERS + rows)
    for i in span["y", 0]:
        if i in own:
            values = [y[0][f].row(i) for f in range(FIELDS)]
            keep_basis(0, i, values)
            for f in range(FIELDS):
                add_products(f, 0, values[f], values[f])
    for level in range(1, ITERS):
        for i in span["y", level]:
            edges = w_dep.row(i), w_col.row(i), w_row.row(i), w_row.row(i - 1)
            olds = [y[level - 1][f].row(i) for f in range(FIELDS)]
            news = [neighbour_sum(olds[f], y[level - 1][f], i, *edges) for f in range(FIELDS)]
            for t, p in every:
                for f in range(FIELDS):
                    y[level][f].put(i, p, t, news[f](p, t))
            if i in own:
                keep_basis(level, i, news)
                for f in range(FIELDS):
                    add_products(f, 2 * level - 1, olds[f], news[f])
                    add_products(f, 2 * level, news[f], news[f])
    for i in span["edge"]:
        dep, col, row = w_dep.row(i), w_col.row(i), w_row.row(i)
        for f in range(FIELDS):
            v, below = y[ITERS - 1][f].row(i), y[ITERS - 1][f].row(i + 1)
            beyond = shifted(v, 1)

            def forward(p, t, v=v, below=below, beyond=beyond):
                lower = v(1, t) if p == 0 else next_sub(v(0, t))
                return dep(p, t) * lower + col(p, t) * beyond(p, t) + row(p, t) * below(p, t)

            add_products(f, MOMENTS - 1, once(forward), v)
    return sums


def halo_tile(lane, before, before_at, after, after_at):
    after_tile = pltpu.roll(after, (LANES - after_at) % LANES, 1) if after_at else after
    shift = (LANES - 8 - before_at) % LANES
    before_tile = pltpu.roll(before, shift, 1) if shift else before
    return jnp.where(lane < 8, after_tile, jnp.where(lane >= LANES - 8, before_tile, 0.0))


def tiles_of(slab, halo):
    cols = slab.shape[-1]
    return [slab[:, at : at + LANES] for at in range(0, cols, LANES)] + [halo]


def corner_tile(lane, ref, kind, parity, row):
    tile = ref[kind, parity]
    place = (8 * row) % (LANES // 2)
    return halo_tile(lane, tile, LANES // 2 + place, tile, place)


def make_stores(rows, refs, earlier=None):
    table = extents(rows)
    stores = {}

    def add(key, name, ref, lead=()):
        first, mid, _ = table[name]
        if earlier is None:
            stores[key] = Rows(ref, first, lead)
        else:
            stores[key] = Rows(ref, mid, lead, earlier.get(key))

    for name in ("image", *WEIGHTS):
        add(name, name, refs[name])
    for f in range(FIELDS):
        add(("mark", f), "mark", refs["mark"], (f,))
        for level in range(ITERS):
            add(("y", level, f), ("y", level), refs["y", level], (f,))
    return stores


STATE = ("image", "mark", *WEIGHTS, *(("y", level) for level in range(ITERS)))


def first_kernel(rows, half, own, label, above, from_left, from_right, corner_above, *refs):
    state = dict(zip(STATE, refs))
    basis, partial = refs[len(STATE) :]

    def fetch(source, kind, before, above_first):
        def parts(i, p, lane):
            row = i - before
            if row < 0:
                halo = corner_tile(lane, corner_above, kind, p, rows + row)
                return tiles_of(above.at[above_first + i, p], halo)
            halo = halo_tile(lane, from_left[kind, p], 8 * row, from_right[kind, p], 8 * row)
            return tiles_of(source.at[row, p], halo)

        return parts

    sums = sweep(
        rows,
        half,
        False,
        fetch(own, 0, IMG_BEFORE, 0),
        fetch(label, 1, SEED_BEFORE, IMG_BEFORE),
        make_stores(rows, state),
        basis,
        0,
        [[None] * MOMENTS] * FIELDS,
    )
    for f in range(FIELDS):
        for k in range(MOMENTS):
            partial[f, k] = sums[f][k]


def second_kernel(rows, half, below, corner_below, *refs):
    earlier = make_stores(rows, dict(zip(STATE, refs)))
    partial = refs[len(STATE)]
    basis, stats = refs[len(STATE) + 1 : len(STATE) + 3]
    state = dict(zip(STATE, refs[len(STATE) + 3 :]))

    def fetch(kind, before, below_first):
        def parts(i, p, lane):
            row = i - before - rows
            return tiles_of(
                below.at[below_first + row, p], corner_tile(lane, corner_below, kind, p, row)
            )

        return parts

    sums = sweep(
        rows,
        half,
        True,
        fetch(0, IMG_BEFORE, 0),
        fetch(1, SEED_BEFORE, IMG_AFTER),
        make_stores(rows, state, earlier),
        basis,
        rows + 2 - 2 * ITERS,
        [[partial[f, k] for k in range(MOMENTS)] for f in range(FIELDS)],
    )
    one_lane = lax.broadcasted_iota(jnp.int32, (1, LANES), 1)
    packed = jnp.zeros((1, LANES), jnp.float32)
    for f in range(FIELDS):
        for k, part in enumerate(sums[f]):
            part = 2.0 * part if k == MOMENTS - 1 else part
            value = jnp.sum(jnp.sum(part, axis=0, keepdims=True), axis=1, keepdims=True)
            packed = jnp.where(one_lane == f * MOMENTS + k, value, packed)
    stats[...] = packed


def combine(a, b):
    out = [None] * (len(a) + len(b) - 1)
    for i, x in enumerate(a):
        for j, z in enumerate(b):
            out[i + j] = x * z if out[i + j] is None else out[i + j] + x * z
    return out


def weighted(coefs, values):
    total = coefs[0] * values[0]
    for c, v in zip(coefs[1:], values[1:]):
        total = total + c * v
    return total


def krylov_coefs(m):
    gaps = [m[k] - m[k + 1] for k in range(MOMENTS - 1)]
    one = jnp.ones_like(m[0])
    zero = jnp.zeros_like(m[0])
    resid, direct, result = [one], [one], [zero] * ITERS
    rz = m[0]
    for k in range(ITERS):
        curve = weighted(combine(direct, direct), gaps)
        alpha = jnp.where(curve > 0.0, rz / curve, 0.0)
        result = [
            result[i] + alpha * direct[i] if i < len(direct) else result[i] for i in range(ITERS)
        ]
        if k + 1 == ITERS:
            break
        image = [
            (direct[i] if i < len(direct) else zero) - (direct[i - 1] if i > 0 else zero)
            for i in range(len(direct) + 1)
        ]
        resid = [(resid[i] if i < len(resid) else zero) - alpha * image[i] for i in range(len(image))]
        rz_next = weighted(combine(resid, resid), m)
        ratio = jnp.where(rz > 0.0, rz_next / rz, 0.0)
        direct = [
            resid[i] + ratio * direct[i] if i < len(direct) else resid[i] for i in range(len(resid))
        ]
        rz = rz_next
    return result


def finish_kernel(rows, half, gathered, basis_one, basis_two, label, out_hbm, out, out_sem):
    core_tiles = out.shape[1]
    total = jnp.sum(gathered[...], axis=0, keepdims=True)
    one_lane = lax.broadcasted_iota(jnp.int32, (1, LANES), 1)
    coefs = []
    for f in range(FIELDS):
        moments = []
        for k in range(MOMENTS):
            pick = jnp.where(one_lane == f * MOMENTS + k, total, 0.0)
            value = jnp.sum(pick, axis=1, keepdims=True)
            moments.append(jnp.broadcast_to(value, (half, LANES)))
        coefs.append(krylov_coefs(moments))
    depth_rows = 2 * half * rows
    second_first = rows + 2 - 2 * ITERS
    copies = []
    for f in range(FIELDS):
        for t in range(core_tiles):
            at = slice(t * LANES, (t + 1) * LANES)
            for row in range(rows):
                for parity in range(2):
                    parts = []
                    for k in range(ITERS):
                        first, mid, _ = extents(rows)["y", k]
                        if row + ITERS < mid:
                            parts.append(basis_one[k, f, row, parity, :, at])
                        else:
                            parts.append(basis_two[k, f, row - second_first, parity, :, at])
                    x = weighted(coefs[f], parts)
                    hit = label[row, parity, :, at] == f + 1.0
                    index = pl.ds(row + rows * parity, half, 2 * rows)
                    out[f, t, index, :] = x + hit.astype(jnp.float32)
            copy = pltpu.make_async_copy(
                out.at[f, t],
                out_hbm.at[pl.ds(f * depth_rows, depth_rows), pl.ds(t * LANES, LANES)],
                out_sem.at[f, t],
            )
            copy.start()
            copies.append(copy)
    for copy in copies:
        copy.wait()


def vmem(count):
    return [pl.BlockSpec(memory_space=pltpu.VMEM)] * count


def hbm(count):
    return [pl.BlockSpec(memory_space=pltpu.HBM)] * count


def on_device(image, seeds):
    depth, rows, cols = image.shape
    half = depth // 2
    wide = cols + LANES
    core_tiles = cols // LANES
    f32 = jnp.float32

    def call(kernel, name, shapes, raw, operands, scratch=(), raw_out=False, mib=16, cost=None):
        return pl.pallas_call(
            lambda *refs: kernel(rows, half, *refs),
            out_shape=[jax.ShapeDtypeStruct(shape, f32) for shape in shapes],
            in_specs=hbm(len(raw)) + vmem(len(operands)),
            out_specs=hbm(len(shapes)) if raw_out else vmem(len(shapes)),
            scratch_shapes=list(scratch),
            compiler_params=pltpu.CompilerParams(vmem_limit_bytes=mib * 1024 * 1024),
            cost_estimate=cost,
            name=name,
        )(*raw, *operands)

    def forward(x, axis):
        return lax.ppermute(x, axis, [(i, i + 1) for i in range(lax.axis_size(axis) - 1)])

    def backward(x, axis):
        return lax.ppermute(x, axis, [(i + 1, i) for i in range(lax.axis_size(axis) - 1)])

    def staged(dtype):
        return pltpu.VMEM((core_tiles, depth * rows, LANES), dtype)

    slabs = (rows, 2, half, cols)
    up, down, own, label = call(
        rows_kernel,
        "own_rows",
        [(UP,) + slabs[1:], (DOWN,) + slabs[1:], slabs, slabs],
        tuple(
            pltpu.with_memory_space_constraint(v.reshape(depth * rows, cols), pltpu.HBM)
            for v in (image, seeds)
        ),
        (),
        [staged(f32), staged(jnp.int32)] + [pltpu.SemaphoreType.DMA((core_tiles,))] * 2,
    )
    above = forward(up, "gy")
    below = backward(down, "gy")
    side = (2, 2, half, LANES)
    even = lax.rem(lax.axis_index("gz"), 2) == 0

    def swap_columns(own, label):
        pair, cross = call(cols_kernel, "own_columns", [side, side], (), (own, label))
        count = lax.axis_size("gz")
        within = [(i, i ^ 1) for i in range(count) if i ^ 1 < count]
        between = [(i, i + 1) for i in range(1, count - 1, 2)]
        pair = lax.ppermute(pair, "gz", within)
        cross = lax.ppermute(cross, "gz", between + [(j, i) for i, j in between])
        left, right = jnp.where(even, cross, pair), jnp.where(even, pair, cross)
        mid = LANES // 2
        corner_up = jnp.concatenate([right[..., mid:], left[..., mid:]], axis=-1)
        corner_down = jnp.concatenate([right[..., :mid], left[..., :mid]], axis=-1)
        return pair, cross, corner_up, corner_down

    def exchange_columns(own, label):
        return swap_columns(own, label)

    pair, cross, corner_up, corner_down = exchange_columns(own, label)
    from_left, from_right = jnp.where(even, cross, pair), jnp.where(even, pair, cross)
    corner_above = forward(corner_up, "gy")
    corner_below = backward(corner_down, "gy")

    table = extents(rows)

    def state_shapes(second):
        shapes = []
        for name in STATE:
            first, mid, stop = table[name]
            count = stop - mid if second else mid - first
            lead = () if name == "image" or name in WEIGHTS else (FIELDS,)
            shapes.append(lead + (count, 2, half, wide))
        return shapes

    second_first = rows + 2 - 2 * ITERS
    basis_rows = (rows + 1 - ITERS, rows - second_first)
    *state, basis_one, partial = call(
        first_kernel,
        "krylov_one",
        state_shapes(False)
        + [(ITERS, FIELDS, basis_rows[0]) + slabs[1:], (FIELDS, MOMENTS, half, LANES)],
        (),
        (own, label, above, from_left, from_right, corner_above),
        cost=pl.CostEstimate(flops=0, bytes_accessed=16 << 20, transcendentals=0),
    )
    basis_two, stats = call(
        second_kernel,
        "krylov_two",
        [(ITERS, FIELDS, basis_rows[1]) + slabs[1:], (1, LANES)],
        (),
        (below, corner_below, *state, partial),
        [pltpu.VMEM(shape, f32) for shape in state_shapes(True)],
    )
    devices = lax.axis_size("gy") * lax.axis_size("gz")
    spread = jnp.broadcast_to(stats[None], (devices, 1, LANES))
    gathered = lax.all_to_all(spread, ("gy", "gz"), 0, 0).reshape(devices, LANES)
    (out,) = call(
        finish_kernel,
        "finish",
        [(FIELDS * depth * rows, cols)],
        (),
        (gathered, basis_one, basis_two, label),
        [
            pltpu.VMEM((FIELDS, core_tiles, depth * rows, LANES), f32),
            pltpu.SemaphoreType.DMA((FIELDS, core_tiles)),
        ],
        raw_out=True,
    )
    return out.reshape(FIELDS, depth, rows, cols)


def solution(mesh):
    return jax.shard_map(
        on_device,
        mesh=mesh,
        in_specs=(P(None, "gy", "gz"), P(None, "gy", "gz")),
        out_specs=P(None, None, "gy", "gz"),
        check_vma=False,
    )
```

```python
import math

import jax
import jax.numpy as jnp
from jax import lax
from jax.experimental import pallas as pl
from jax.experimental.pallas import tpu as pltpu
from jax.sharding import PartitionSpec as P

ITERS = 4
FIELDS = 2
EDGE_BETA = 60.0
EDGE_FLOOR = 0.05
LANES = 128

IMG_BEFORE, IMG_AFTER = ITERS + 2, ITERS + 3
SEED_BEFORE, SEED_AFTER = ITERS, ITERS + 1
UP = IMG_BEFORE + SEED_BEFORE
DOWN = IMG_AFTER + SEED_AFTER
MOMENTS = 2 * ITERS
MIDDLE_COST = 10


def gauss_taps():
    raw = [math.exp(-0.5 * k * k) for k in range(-2, 3)]
    total = sum(raw)
    return [value / total for value in raw]


def slab_of(ref, row, parity, rows, half):
    index = pl.ds(row + rows * parity, half, 2 * rows)
    return jnp.concatenate([ref[t, index, :] for t in range(ref.shape[0])], axis=1)


def stage(pairs):
    copies = [
        pltpu.make_async_copy(source.at[:, pl.ds(t * LANES, LANES)], staged.at[t], sems.at[t])
        for source, staged, sems in pairs
        for t in range(staged.shape[0])
    ]
    for copy in copies:
        copy.start()
    for copy in copies:
        copy.wait()


def rows_kernel(rows, half, image_hbm, seeds_hbm, up, down, own, label, image, seeds, image_sem, seeds_sem):
    stage([(image_hbm, image, image_sem), (seeds_hbm, seeds, seeds_sem)])
    for row in range(rows):
        for parity in range(2):
            grey = slab_of(image, row, parity, rows, half)
            seed = slab_of(seeds, row, parity, rows, half).astype(jnp.float32)
            own[row, parity] = grey
            label[row, parity] = seed
            if row >= rows - IMG_BEFORE:
                up[row - (rows - IMG_BEFORE), parity] = grey
            if row >= rows - SEED_BEFORE:
                up[IMG_BEFORE + row - (rows - SEED_BEFORE), parity] = seed
            if row < IMG_AFTER:
                down[row, parity] = grey
            if row < SEED_AFTER:
                down[IMG_AFTER + row, parity] = seed


def cols_kernel(rows, half, own, label, pair, cross):
    even = lax.rem(lax.axis_index("gz"), 2) == 0
    cols = own.shape[3]
    lane = lax.broadcasted_iota(jnp.int32, (half, LANES), 1)
    for kind, source in enumerate((own, label)):
        for parity in range(2):
            head = jnp.zeros((half, LANES), jnp.float32)
            tail = jnp.zeros((half, LANES), jnp.float32)
            for row in range(rows):
                first = source[row, parity, :, 0:LANES]
                last = source[row, parity, :, cols - LANES : cols]
                here = (lane >= 8 * row) & (lane < 8 * row + 8)
                shift = (8 * row) % LANES
                head = jnp.where(here, pltpu.roll(first, shift, 1) if shift else first, head)
                shift = (8 * row + 8) % LANES
                tail = jnp.where(here, pltpu.roll(last, shift, 1) if shift else last, tail)
            pair[kind, parity] = jnp.where(even, tail, head)
            cross[kind, parity] = jnp.where(even, head, tail)


def once(get):
    known = {}

    def value(parity, t):
        if (parity, t) not in known:
            known[parity, t] = get(parity, t)
        return known[parity, t]

    return value


class Rows:
    def __init__(self, pieces, lead=()):
        self.pieces, self.lead = pieces, lead

    def place(self, start, i, parity, t):
        lanes = slice(t * LANES, (t + 1) * LANES)
        return (*self.lead, i - start, parity, slice(None), lanes)

    def row(self, i):
        for span, ref in self.pieces:
            if i in span:
                return once(lambda parity, t: ref[self.place(span.start, i, parity, t)])
        raise IndexError(i)

    def put(self, i, parity, t, value):
        span, ref = self.pieces[0]
        if i not in span:
            raise IndexError(i)
        ref[self.place(span.start, i, parity, t)] = value


MIDDLE, HEAD, TAIL = range(3)
WEIGHTS = ("smooth", "w_raw", "d_raw", "c_raw", "scale", "w_row", "w_dep", "w_col")


def extents(rows, part):
    low = IMG_BEFORE
    table = {
        "image": (0, low, rows + IMG_BEFORE, rows + IMG_BEFORE + IMG_AFTER),
        "mark": (0, SEED_BEFORE, rows + SEED_BEFORE, rows + SEED_BEFORE + SEED_AFTER),
        "smooth": (0, low, rows + 2, rows + 2 * ITERS + 1),
        "w_raw": (0, low, rows + 1, rows + 2 * ITERS),
        "d_raw": (1, low, rows + 2, rows + 2 * ITERS),
        "c_raw": (1, low, rows + 2, rows + 2 * ITERS),
        "scale": (1, low + 1, rows + 1, rows + 2 * ITERS),
        "w_row": (1, low + 1, rows, rows + 2 * ITERS - 1),
        "w_dep": (2, low + 1, rows + 1, rows + 2 * ITERS - 1),
        "w_col": (2, low + 1, rows + 1, rows + 2 * ITERS - 1),
        "edge": (ITERS, low + ITERS, rows + 1 - ITERS, rows + ITERS),
    }
    for level in range(ITERS):
        table["y", level] = (1 + level, low + 1 + level, rows + 1 - level, rows + 2 * ITERS - level)
    return {
        name: (range(low, high), range(first, low), range(high, stop))[part]
        for name, (first, low, high, stop) in table.items()
    }


def basis_span(rows, part):
    spans = [extents(rows, part)["y", level] for level in range(ITERS)]
    first = max(min(span.start for span in spans), ITERS)
    return range(first - ITERS, min(max(span.stop for span in spans), rows + ITERS) - ITERS)


def sweep(rows, half, part, fetch_image, fetch_seeds, stores, basis, partial):
    span = extents(rows, part)
    basis_first = basis_span(rows, part).start
    tiles = stores["smooth"].pieces[0][1].shape[-1] // LANES
    core_tiles = tiles - 1
    gy, gz = lax.axis_index("gy"), lax.axis_index("gz")
    last_gy, last_gz = lax.axis_size("gy") - 1, lax.axis_size("gz") - 1
    t0, t1, t2 = gauss_taps()[:3]
    lane = lax.broadcasted_iota(jnp.int32, (half, LANES), 1)
    sub = lax.broadcasted_iota(jnp.int32, (half, LANES), 0)
    not_first = (sub > 0).astype(jnp.float32)
    not_last = (sub < half - 1).astype(jnp.float32)
    every = [(t, p) for t in range(tiles) for p in range(2)]
    inner = [(t, p) for t in range(core_tiles) for p in range(2)]

    def shifted(get, by):
        turned = once(lambda parity, t: pltpu.roll(get(parity, t), -by % LANES, 1))
        if by > 0:
            return once(
                lambda parity, t: jnp.where(
                    lane < LANES - by, turned(parity, t), turned(parity, (t + 1) % tiles)
                )
            )
        return once(
            lambda parity, t: jnp.where(lane >= -by, turned(parity, t), turned(parity, (t - 1) % tiles))
        )

    def next_sub(v):
        return pltpu.roll(v, half - 1, 0)

    def prev_sub(v):
        return pltpu.roll(v, 1, 0)

    image, smooth, scale = stores["image"], stores["smooth"], stores["scale"]
    w_raw, d_raw, c_raw = stores["w_raw"], stores["d_raw"], stores["c_raw"]
    w_row, w_dep, w_col = stores["w_row"], stores["w_dep"], stores["w_col"]
    marks = [stores["mark", f] for f in range(FIELDS)]
    y = [[stores["y", level, f] for f in range(FIELDS)] for level in range(ITERS)]

    for i in span["image"]:
        for p in range(2):
            for t, part in enumerate(fetch_image(i, p, lane)):
                image.put(i, p, t, part)
    for i in span["mark"]:
        for p in range(2):
            for t, part in enumerate(fetch_seeds(i, p, lane)):
                for f in range(FIELDS):
                    marks[f].put(i, p, t, (part == f + 1.0).astype(jnp.float32))

    for i in span["smooth"]:
        x = [image.row(i + k) for k in range(5)]
        flat = once(
            lambda p, t, x=x: t0 * (x[0](p, t) + x[4](p, t))
            + t1 * (x[1](p, t) + x[3](p, t))
            + t2 * x[2](p, t)
        )
        later = once(lambda p, t, flat=flat: not_last * next_sub(flat(p, t)))
        sooner = once(lambda p, t, flat=flat: not_first * prev_sub(flat(p, t)))
        for t, p in every:
            near = flat(1, t) + sooner(1, t) if p == 0 else flat(0, t) + later(0, t)
            smooth.put(i, p, t, t0 * (later(p, t) + sooner(p, t)) + t1 * near + t2 * flat(p, t))
    for i in span["smooth"]:
        deep = smooth.row(i)
        near_next, near_prev = shifted(deep, 1), shifted(deep, -1)
        far_next, far_prev = shifted(deep, 2), shifted(deep, -2)
        fresh = [
            (
                p,
                t,
                t0 * (far_next(p, t) + far_prev(p, t))
                + t1 * (near_next(p, t) + near_prev(p, t))
                + t2 * deep(p, t),
            )
            for t, p in every
        ]
        for p, t, value in fresh:
            smooth.put(i, p, t, value)

    cut_tile = {
        core_tiles - 1: jnp.where((lane == LANES - 1) & (gz == last_gz), 0.0, 1.0),
        tiles - 1: jnp.where((lane == LANES - 1) & (gz == 0), 0.0, 1.0),
    }

    def weight(step):
        return EDGE_FLOOR + jnp.exp((-EDGE_BETA * step) * step)

    cut_row = {
        ITERS - 1: jnp.where(gy == 0, 0.0, 1.0),
        ITERS + rows - 1: jnp.where(gy == last_gy, 0.0, 1.0),
    }
    for i in sorted(set(span["w_raw"]) | set(span["d_raw"])):
        here = smooth.row(i)
        if i in span["w_raw"]:
            after = smooth.row(i + 1)
            for t, p in every:
                value = weight(after(p, t) - here(p, t))
                w_raw.put(i, p, t, cut_row[i] * value if i in cut_row else value)
        if i in span["d_raw"]:
            beyond = shifted(here, 1)
            for t, p in every:
                if p == 0:
                    d_raw.put(i, p, t, weight(here(1, t) - here(0, t)))
                else:
                    d_raw.put(i, p, t, not_last * weight(next_sub(here(0, t)) - here(1, t)))
                value = weight(beyond(p, t) - here(p, t))
                c_raw.put(i, p, t, cut_tile[t] * value if t in cut_tile else value)

    for i in span["scale"]:
        dep, col, down, up = d_raw.row(i), c_raw.row(i), w_raw.row(i), w_raw.row(i - 1)
        col_back = shifted(col, -1)
        seeded = [mark.row(i) for mark in marks]
        for t, p in every:
            back = prev_sub(dep(1, t)) if p == 0 else dep(0, t)
            deg = dep(p, t) + back + down(p, t) + up(p, t) + col(p, t) + col_back(p, t)
            free = seeded[0](p, t) + seeded[1](p, t) == 0.0
            scale.put(i, p, t, jnp.where(free, lax.rsqrt(deg), 0.0))

    def neighbour_sum(v, field, i, dep, col, down, up):
        above, below = field.row(i - 1), field.row(i + 1)
        beyond = shifted(v, 1)
        pushed = shifted(lambda p, t: col(p, t) * v(p, t), -1)

        def total(p, t):
            if p == 0:
                depth = dep(0, t) * v(1, t) + prev_sub(dep(1, t) * v(1, t))
            else:
                depth = dep(1, t) * next_sub(v(0, t)) + dep(0, t) * v(0, t)
            return (depth + (col(p, t) * beyond(p, t) + pushed(p, t))) + (
                down(p, t) * below(p, t) + up(p, t) * above(p, t)
            )

        return once(total)

    for i in span["y", 0]:
        edges = d_raw.row(i), c_raw.row(i), w_raw.row(i), w_raw.row(i - 1)
        s = scale.row(i)
        totals = [neighbour_sum(mark.row(i), mark, i, *edges) for mark in marks]
        for t, p in every:
            for f in range(FIELDS):
                y[0][f].put(i, p, t, s(p, t) * totals[f](p, t))

    for i in sorted(set(span["w_row"]) | set(span["w_dep"])):
        s = scale.row(i)
        if i in span["w_row"]:
            after, down = scale.row(i + 1), w_raw.row(i)
            for t, p in every:
                w_row.put(i, p, t, down(p, t) * s(p, t) * after(p, t))
        if i in span["w_dep"]:
            dep, col = d_raw.row(i), c_raw.row(i)
            beyond = shifted(s, 1)
            for t, p in every:
                other = s(1, t) if p == 0 else next_sub(s(0, t))
                w_dep.put(i, p, t, dep(p, t) * s(p, t) * other)
                w_col.put(i, p, t, col(p, t) * s(p, t) * beyond(p, t))

    sums = [[None] * MOMENTS for _ in range(FIELDS)]

    def add_products(f, k, a, b):
        total = None
        for t, p in inner:
            part = a(p, t) * b(p, t)
            total = part if total is None else total + part
        sums[f][k] = total if sums[f][k] is None else sums[f][k] + total

    def keep_basis(level, i, values):
        s = scale.row(i)
        for t, p in inner:
            for f in range(FIELDS):
                lanes = slice(t * LANES, (t + 1) * LANES)
                basis[level, f, i - ITERS - basis_first, p, :, lanes] = s(p, t) * values[f](p, t)

    own = range(ITERS, ITERS + rows)
    for i in span["y", 0]:
        if i in own:
            values = [y[0][f].row(i) for f in range(FIELDS)]
            keep_basis(0, i, values)
            for f in range(FIELDS):
                add_products(f, 0, values[f], values[f])
    for level in range(1, ITERS):
        for i in span["y", level]:
            edges = w_dep.row(i), w_col.row(i), w_row.row(i), w_row.row(i - 1)
            olds = [y[level - 1][f].row(i) for f in range(FIELDS)]
            news = [neighbour_sum(olds[f], y[level - 1][f], i, *edges) for f in range(FIELDS)]
            for t, p in every:
                for f in range(FIELDS):
                    y[level][f].put(i, p, t, news[f](p, t))
            if i in own:
                keep_basis(level, i, news)
                for f in range(FIELDS):
                    add_products(f, 2 * level - 1, olds[f], news[f])
                    add_products(f, 2 * level, news[f], news[f])
    for i in span["edge"]:
        dep, col, row = w_dep.row(i), w_col.row(i), w_row.row(i)
        for f in range(FIELDS):
            v, below = y[ITERS - 1][f].row(i), y[ITERS - 1][f].row(i + 1)
            beyond = shifted(v, 1)

            def forward(p, t, v=v, below=below, beyond=beyond):
                lower = v(1, t) if p == 0 else next_sub(v(0, t))
                return dep(p, t) * lower + col(p, t) * beyond(p, t) + row(p, t) * below(p, t)

            add_products(f, MOMENTS - 1, once(forward), v)
    for f in range(FIELDS):
        for k in range(MOMENTS):
            partial[f, k] = sums[f][k]


def halo_tile(lane, before, before_at, after, after_at):
    after_tile = pltpu.roll(after, (LANES - after_at) % LANES, 1) if after_at else after
    shift = (LANES - 8 - before_at) % LANES
    before_tile = pltpu.roll(before, shift, 1) if shift else before
    return jnp.where(lane < 8, after_tile, jnp.where(lane >= LANES - 8, before_tile, 0.0))


def tiles_of(slab, halo):
    cols = slab.shape[-1]
    return [slab[:, at : at + LANES] for at in range(0, cols, LANES)] + [halo]


def corner_tile(lane, ref, kind, parity, row):
    tile = ref[kind, parity]
    place = (8 * row) % (LANES // 2)
    return halo_tile(lane, tile, LANES // 2 + place, tile, place)


STATE = ("image", "mark", *WEIGHTS, *(("y", level) for level in range(ITERS)))


def make_stores(rows, *parts):
    stores = {}

    def pieces(name):
        return [(extents(rows, part)[name], refs[STATE.index(name)]) for part, refs in parts]

    for name in ("image", *WEIGHTS):
        stores[name] = Rows(pieces(name))
    for f in range(FIELDS):
        stores["mark", f] = Rows(pieces("mark"), (f,))
        for level in range(ITERS):
            stores["y", level, f] = Rows(pieces(("y", level)), (f,))
    return stores


def middle_kernel(rows, half, own, label, from_left, from_right, *refs):
    state, (basis, partial) = refs[: len(STATE)], refs[len(STATE) :]

    def fetch(source, kind, before):
        def parts(i, p, lane):
            row = i - before
            halo = halo_tile(lane, from_left[kind, p], 8 * row, from_right[kind, p], 8 * row)
            return tiles_of(source.at[row, p], halo)

        return parts

    images, labels = fetch(own, 0, IMG_BEFORE), fetch(label, 1, SEED_BEFORE)
    stores = make_stores(rows, (MIDDLE, state))
    sweep(rows, half, MIDDLE, images, labels, stores, basis, partial)


def head_kernel(rows, half, above, corner_above, *refs):
    count = len(STATE)
    middle, (basis, partial), state = refs[:count], refs[count : count + 2], refs[count + 2 :]

    def fetch(kind, before, first):
        def parts(i, p, lane):
            halo = corner_tile(lane, corner_above, kind, p, rows + i - before)
            return tiles_of(above.at[first + i, p], halo)

        return parts

    images, labels = fetch(0, IMG_BEFORE, 0), fetch(1, SEED_BEFORE, IMG_BEFORE)
    stores = make_stores(rows, (HEAD, state), (MIDDLE, middle))
    sweep(rows, half, HEAD, images, labels, stores, basis, partial)


def tail_kernel(rows, half, below, corner_below, *refs):
    count = len(STATE)
    middle, refs = refs[:count], refs[count:]
    (others, (basis, stats), partial), state = (refs[:2], refs[2:4], refs[4]), refs[5:]

    def fetch(kind, before, first):
        def parts(i, p, lane):
            row = i - before - rows
            halo = corner_tile(lane, corner_below, kind, p, row)
            return tiles_of(below.at[first + row, p], halo)

        return parts

    images, labels = fetch(0, IMG_BEFORE, 0), fetch(1, SEED_BEFORE, IMG_AFTER)
    stores = make_stores(rows, (TAIL, state), (MIDDLE, middle))
    sweep(rows, half, TAIL, images, labels, stores, basis, partial)
    one_lane = lax.broadcasted_iota(jnp.int32, (1, LANES), 1)
    packed = jnp.zeros((1, LANES), jnp.float32)
    for f in range(FIELDS):
        for k in range(MOMENTS):
            whole = partial[f, k] + others[0][f, k] + others[1][f, k]
            whole = 2.0 * whole if k == MOMENTS - 1 else whole
            value = jnp.sum(jnp.sum(whole, axis=0, keepdims=True), axis=1, keepdims=True)
            packed = jnp.where(one_lane == f * MOMENTS + k, value, packed)
    stats[...] = packed


def combine(a, b):
    out = [None] * (len(a) + len(b) - 1)
    for i, x in enumerate(a):
        for j, z in enumerate(b):
            out[i + j] = x * z if out[i + j] is None else out[i + j] + x * z
    return out


def weighted(coefs, values):
    total = coefs[0] * values[0]
    for c, v in zip(coefs[1:], values[1:]):
        total = total + c * v
    return total


def krylov_coefs(m):
    gaps = [m[k] - m[k + 1] for k in range(MOMENTS - 1)]
    one = jnp.ones_like(m[0])
    zero = jnp.zeros_like(m[0])
    resid, direct, result = [one], [one], [zero] * ITERS
    rz = m[0]
    for k in range(ITERS):
        curve = weighted(combine(direct, direct), gaps)
        alpha = jnp.where(curve > 0.0, rz / curve, 0.0)
        result = [
            result[i] + alpha * direct[i] if i < len(direct) else result[i] for i in range(ITERS)
        ]
        if k + 1 == ITERS:
            break
        image = [
            (direct[i] if i < len(direct) else zero) - (direct[i - 1] if i > 0 else zero)
            for i in range(len(direct) + 1)
        ]
        resid = [(resid[i] if i < len(resid) else zero) - alpha * image[i] for i in range(len(image))]
        rz_next = weighted(combine(resid, resid), m)
        ratio = jnp.where(rz > 0.0, rz_next / rz, 0.0)
        direct = [
            resid[i] + ratio * direct[i] if i < len(direct) else resid[i] for i in range(len(resid))
        ]
        rz = rz_next
    return result


def finish_kernel(rows, half, gathered, middle, head, tail, label, out_hbm, out, out_sem):
    core_tiles = out.shape[1]
    total = jnp.sum(gathered[...], axis=0, keepdims=True)
    one_lane = lax.broadcasted_iota(jnp.int32, (1, LANES), 1)
    coefs = []
    for f in range(FIELDS):
        moments = []
        for k in range(MOMENTS):
            pick = jnp.where(one_lane == f * MOMENTS + k, total, 0.0)
            value = jnp.sum(pick, axis=1, keepdims=True)
            moments.append(jnp.broadcast_to(value, (half, LANES)))
        coefs.append(krylov_coefs(moments))
    depth_rows = 2 * half * rows
    copies = []
    for f in range(FIELDS):
        for t in range(core_tiles):
            at = slice(t * LANES, (t + 1) * LANES)
            for row in range(rows):
                for parity in range(2):
                    parts = []
                    for k in range(ITERS):
                        for part, basis in enumerate((middle, head, tail)):
                            if row + ITERS in extents(rows, part)["y", k]:
                                place = row - basis_span(rows, part).start
                                parts.append(basis[k, f, place, parity, :, at])
                    x = weighted(coefs[f], parts)
                    hit = label[row, parity, :, at] == f + 1.0
                    index = pl.ds(row + rows * parity, half, 2 * rows)
                    out[f, t, index, :] = x + hit.astype(jnp.float32)
            copy = pltpu.make_async_copy(
                out.at[f, t],
                out_hbm.at[pl.ds(f * depth_rows, depth_rows), pl.ds(t * LANES, LANES)],
                out_sem.at[f, t],
            )
            copy.start()
            copies.append(copy)
    for copy in copies:
        copy.wait()


def vmem(count):
    return [pl.BlockSpec(memory_space=pltpu.VMEM)] * count


def hbm(count):
    return [pl.BlockSpec(memory_space=pltpu.HBM)] * count


def on_device(image, seeds):
    depth, rows, cols = image.shape
    half = depth // 2
    wide = cols + LANES
    core_tiles = cols // LANES
    f32 = jnp.float32

    def call(kernel, name, shapes, raw, operands, scratch=(), raw_out=False, mib=16, cost=None):
        return pl.pallas_call(
            lambda *refs: kernel(rows, half, *refs),
            out_shape=[jax.ShapeDtypeStruct(shape, f32) for shape in shapes],
            in_specs=hbm(len(raw)) + vmem(len(operands)),
            out_specs=hbm(len(shapes)) if raw_out else vmem(len(shapes)),
            scratch_shapes=list(scratch),
            compiler_params=pltpu.CompilerParams(vmem_limit_bytes=mib * 1024 * 1024),
            cost_estimate=cost,
            name=name,
        )(*raw, *operands)

    def forward(x, axis):
        return lax.ppermute(x, axis, [(i, i + 1) for i in range(lax.axis_size(axis) - 1)])

    def backward(x, axis):
        return lax.ppermute(x, axis, [(i + 1, i) for i in range(lax.axis_size(axis) - 1)])

    def staged(dtype):
        return pltpu.VMEM((core_tiles, depth * rows, LANES), dtype)

    slabs = (rows, 2, half, cols)
    up, down, own, label = call(
        rows_kernel,
        "own_rows",
        [(UP,) + slabs[1:], (DOWN,) + slabs[1:], slabs, slabs],
        tuple(
            pltpu.with_memory_space_constraint(v.reshape(depth * rows, cols), pltpu.HBM)
            for v in (image, seeds)
        ),
        (),
        [staged(f32), staged(jnp.int32)] + [pltpu.SemaphoreType.DMA((core_tiles,))] * 2,
    )
    above = forward(up, "gy")
    below = backward(down, "gy")
    side = (2, 2, half, LANES)
    even = lax.rem(lax.axis_index("gz"), 2) == 0

    def swap_columns(own, label):
        pair, cross = call(cols_kernel, "own_columns", [side, side], (), (own, label))
        count = lax.axis_size("gz")
        within = [(i, i ^ 1) for i in range(count) if i ^ 1 < count]
        between = [(i, i + 1) for i in range(1, count - 1, 2)]
        pair = lax.ppermute(pair, "gz", within)
        cross = lax.ppermute(cross, "gz", between + [(j, i) for i, j in between])
        left, right = jnp.where(even, cross, pair), jnp.where(even, pair, cross)
        mid = LANES // 2
        corner_up = jnp.concatenate([right[..., mid:], left[..., mid:]], axis=-1)
        corner_down = jnp.concatenate([right[..., :mid], left[..., :mid]], axis=-1)
        return pair, cross, corner_up, corner_down

    def exchange_columns(own, label):
        return swap_columns(own, label)

    pair, cross, corner_up, corner_down = exchange_columns(own, label)
    from_left, from_right = jnp.where(even, cross, pair), jnp.where(even, pair, cross)
    corner_above = forward(corner_up, "gy")
    corner_below = backward(corner_down, "gy")

    def state_shapes(part):
        shapes = []
        for name in STATE:
            lead = () if name == "image" or name in WEIGHTS else (FIELDS,)
            shapes.append(lead + (len(extents(rows, part)[name]), 2, half, wide))
        return shapes

    def basis_shape(part):
        return (ITERS, FIELDS, len(basis_span(rows, part))) + slabs[1:]

    def scratch(part):
        return [pltpu.VMEM(shape, f32) for shape in state_shapes(part)]

    sums = (FIELDS, MOMENTS, half, LANES)
    *state, basis_middle, sums_middle = call(
        middle_kernel,
        "middle",
        state_shapes(MIDDLE) + [basis_shape(MIDDLE), sums],
        (),
        (own, label, from_left, from_right),
        cost=pl.CostEstimate(flops=0, bytes_accessed=MIDDLE_COST << 20, transcendentals=0),
    )
    basis_head, sums_head = call(
        head_kernel,
        "head",
        [basis_shape(HEAD), sums],
        (),
        (above, corner_above, *state),
        scratch(HEAD),
        cost=pl.CostEstimate(flops=0, bytes_accessed=8 << 20, transcendentals=0),
    )
    basis_tail, stats = call(
        tail_kernel,
        "tail",
        [basis_shape(TAIL), (1, LANES)],
        (),
        (below, corner_below, *state, sums_middle, sums_head),
        [pltpu.VMEM(sums, f32)] + scratch(TAIL),
    )
    devices = lax.axis_size("gy") * lax.axis_size("gz")
    spread = jnp.broadcast_to(stats[None], (devices, 1, LANES))
    gathered = lax.all_to_all(spread, ("gy", "gz"), 0, 0).reshape(devices, LANES)
    (out,) = call(
        finish_kernel,
        "finish",
        [(FIELDS * depth * rows, cols)],
        (),
        (gathered, basis_middle, basis_head, basis_tail, label),
        [
            pltpu.VMEM((FIELDS, core_tiles, depth * rows, LANES), f32),
            pltpu.SemaphoreType.DMA((FIELDS, core_tiles)),
        ],
        raw_out=True,
    )
    return out.reshape(FIELDS, depth, rows, cols)


def solution(mesh):
    return jax.shard_map(
        on_device,
        mesh=mesh,
        in_specs=(P(None, "gy", "gz"), P(None, "gy", "gz")),
        out_specs=P(None, None, "gy", "gz"),
        check_vma=False,
    )
```

```python
import math

import jax
import jax.numpy as jnp
from jax import lax
from jax.experimental import pallas as pl
from jax.experimental.pallas import tpu as pltpu
from jax.sharding import PartitionSpec as P

ITERS = 4
FIELDS = 2
EDGE_BETA = 60.0
EDGE_FLOOR = 0.05
LANES = 128

IMG_BEFORE, IMG_AFTER = ITERS + 2, ITERS + 3
SEED_BEFORE, SEED_AFTER = ITERS, ITERS + 1
UP = IMG_BEFORE + SEED_BEFORE
DOWN = IMG_AFTER + SEED_AFTER
MOMENTS = 2 * ITERS
MIDDLE_COST = 10


def gauss_taps():
    raw = [math.exp(-0.5 * k * k) for k in range(-2, 3)]
    total = sum(raw)
    return [value / total for value in raw]


def rows_kernel(rows, half, image_hbm, seeds_hbm, up, down, own, label, image, seeds, image_sem, seeds_sem):
    sources = ((image_hbm, image, image_sem), (seeds_hbm, seeds, seeds_sem))
    copies = [
        [
            pltpu.make_async_copy(source.at[:, pl.ds(t * LANES, LANES)], staged.at[t], sems.at[t])
            for source, staged, sems in sources
        ]
        for t in range(image.shape[0])
    ]
    for pair in copies:
        for copy in pair:
            copy.start()
    for t, pair in enumerate(copies):
        at = slice(t * LANES, (t + 1) * LANES)
        for copy in pair:
            copy.wait()
        for row in range(rows):
            for parity in range(2):
                index = pl.ds(row + rows * parity, half, 2 * rows)
                grey = image[t, index, :]
                seed = seeds[t, index, :].astype(jnp.float32)
                own[row, parity, :, at] = grey
                label[row, parity, :, at] = seed
                if row >= rows - IMG_BEFORE:
                    up[row - (rows - IMG_BEFORE), parity, :, at] = grey
                if row >= rows - SEED_BEFORE:
                    up[IMG_BEFORE + row - (rows - SEED_BEFORE), parity, :, at] = seed
                if row < IMG_AFTER:
                    down[row, parity, :, at] = grey
                if row < SEED_AFTER:
                    down[IMG_AFTER + row, parity, :, at] = seed


def cols_kernel(rows, half, own, label, pair, cross):
    even = lax.rem(lax.axis_index("gz"), 2) == 0
    cols = own.shape[3]
    lane = lax.broadcasted_iota(jnp.int32, (half, LANES), 1)
    for kind, source in enumerate((own, label)):
        for parity in range(2):
            head = jnp.zeros((half, LANES), jnp.float32)
            tail = jnp.zeros((half, LANES), jnp.float32)
            for row in range(rows):
                first = source[row, parity, :, 0:LANES]
                last = source[row, parity, :, cols - LANES : cols]
                here = (lane >= 8 * row) & (lane < 8 * row + 8)
                shift = (8 * row) % LANES
                head = jnp.where(here, pltpu.roll(first, shift, 1) if shift else first, head)
                shift = (8 * row + 8) % LANES
                tail = jnp.where(here, pltpu.roll(last, shift, 1) if shift else last, tail)
            pair[kind, parity] = jnp.where(even, tail, head)
            cross[kind, parity] = jnp.where(even, head, tail)


def once(get):
    known = {}

    def value(parity, t):
        if (parity, t) not in known:
            known[parity, t] = get(parity, t)
        return known[parity, t]

    return value


class Rows:
    def __init__(self, pieces, lead=()):
        self.pieces, self.lead = pieces, lead

    def place(self, start, i, parity, t):
        lanes = slice(t * LANES, (t + 1) * LANES)
        return (*self.lead, i - start, parity, slice(None), lanes)

    def row(self, i):
        for span, ref in self.pieces:
            if i in span:
                return once(lambda parity, t: ref[self.place(span.start, i, parity, t)])
        raise IndexError(i)

    def put(self, i, parity, t, value):
        span, ref = self.pieces[0]
        if i not in span:
            raise IndexError(i)
        ref[self.place(span.start, i, parity, t)] = value


MIDDLE, HEAD, TAIL = range(3)
WEIGHTS = ("smooth", "w_raw", "d_raw", "c_raw", "scale", "w_row", "w_dep", "w_col")


def extents(rows, part):
    low = IMG_BEFORE
    table = {
        "image": (0, low, rows + IMG_BEFORE, rows + IMG_BEFORE + IMG_AFTER),
        "mark": (0, SEED_BEFORE, rows + SEED_BEFORE, rows + SEED_BEFORE + SEED_AFTER),
        "smooth": (0, low, rows + 2, rows + 2 * ITERS + 1),
        "w_raw": (0, low, rows + 1, rows + 2 * ITERS),
        "d_raw": (1, low, rows + 2, rows + 2 * ITERS),
        "c_raw": (1, low, rows + 2, rows + 2 * ITERS),
        "scale": (1, low + 1, rows + 1, rows + 2 * ITERS),
        "w_row": (1, low + 1, rows, rows + 2 * ITERS - 1),
        "w_dep": (2, low + 1, rows + 1, rows + 2 * ITERS - 1),
        "w_col": (2, low + 1, rows + 1, rows + 2 * ITERS - 1),
        "edge": (ITERS, low + ITERS, rows + 1 - ITERS, rows + ITERS),
    }
    for level in range(ITERS):
        table["y", level] = (1 + level, low + 1 + level, rows + 1 - level, rows + 2 * ITERS - level)
    return {
        name: (range(low, high), range(first, low), range(high, stop))[part]
        for name, (first, low, high, stop) in table.items()
    }


def basis_span(rows, part):
    spans = [extents(rows, part)["y", level] for level in range(ITERS)]
    first = max(min(span.start for span in spans), ITERS)
    return range(first - ITERS, min(max(span.stop for span in spans), rows + ITERS) - ITERS)


def sweep(rows, half, part, fetch_image, fetch_seeds, stores, basis, partial):
    span = extents(rows, part)
    basis_first = basis_span(rows, part).start
    tiles = stores["smooth"].pieces[0][1].shape[-1] // LANES
    core_tiles = tiles - 1
    gy, gz = lax.axis_index("gy"), lax.axis_index("gz")
    last_gy, last_gz = lax.axis_size("gy") - 1, lax.axis_size("gz") - 1
    t0, t1, t2 = gauss_taps()[:3]
    lane = lax.broadcasted_iota(jnp.int32, (half, LANES), 1)
    sub = lax.broadcasted_iota(jnp.int32, (half, LANES), 0)
    not_first = (sub > 0).astype(jnp.float32)
    not_last = (sub < half - 1).astype(jnp.float32)
    every = [(t, p) for t in range(tiles) for p in range(2)]
    inner = [(t, p) for t in range(core_tiles) for p in range(2)]

    def shifted(get, by):
        turned = once(lambda parity, t: pltpu.roll(get(parity, t), -by % LANES, 1))
        if by > 0:
            return once(
                lambda parity, t: jnp.where(
                    lane < LANES - by, turned(parity, t), turned(parity, (t + 1) % tiles)
                )
            )
        return once(
            lambda parity, t: jnp.where(lane >= -by, turned(parity, t), turned(parity, (t - 1) % tiles))
        )

    def next_sub(v):
        return pltpu.roll(v, half - 1, 0)

    def prev_sub(v):
        return pltpu.roll(v, 1, 0)

    image, smooth, scale = stores["image"], stores["smooth"], stores["scale"]
    w_raw, d_raw, c_raw = stores["w_raw"], stores["d_raw"], stores["c_raw"]
    w_row, w_dep, w_col = stores["w_row"], stores["w_dep"], stores["w_col"]
    marks = [stores["mark", f] for f in range(FIELDS)]
    y = [[stores["y", level, f] for f in range(FIELDS)] for level in range(ITERS)]

    for i in span["image"]:
        for p in range(2):
            for t, part in enumerate(fetch_image(i, p, lane)):
                image.put(i, p, t, part)
    for i in span["mark"]:
        for p in range(2):
            for t, part in enumerate(fetch_seeds(i, p, lane)):
                for f in range(FIELDS):
                    marks[f].put(i, p, t, (part == f + 1.0).astype(jnp.float32))

    for i in span["smooth"]:
        x = [image.row(i + k) for k in range(5)]
        flat = once(
            lambda p, t, x=x: t0 * (x[0](p, t) + x[4](p, t))
            + t1 * (x[1](p, t) + x[3](p, t))
            + t2 * x[2](p, t)
        )
        later = once(lambda p, t, flat=flat: not_last * next_sub(flat(p, t)))
        sooner = once(lambda p, t, flat=flat: not_first * prev_sub(flat(p, t)))
        for t, p in every:
            near = flat(1, t) + sooner(1, t) if p == 0 else flat(0, t) + later(0, t)
            smooth.put(i, p, t, t0 * (later(p, t) + sooner(p, t)) + t1 * near + t2 * flat(p, t))
    for i in span["smooth"]:
        deep = smooth.row(i)
        near_next, near_prev = shifted(deep, 1), shifted(deep, -1)
        far_next, far_prev = shifted(deep, 2), shifted(deep, -2)
        fresh = [
            (
                p,
                t,
                t0 * (far_next(p, t) + far_prev(p, t))
                + t1 * (near_next(p, t) + near_prev(p, t))
                + t2 * deep(p, t),
            )
            for t, p in every
        ]
        for p, t, value in fresh:
            smooth.put(i, p, t, value)

    cut_tile = {
        core_tiles - 1: jnp.where((lane == LANES - 1) & (gz == last_gz), 0.0, 1.0),
        tiles - 1: jnp.where((lane == LANES - 1) & (gz == 0), 0.0, 1.0),
    }

    def weight(step):
        return EDGE_FLOOR + jnp.exp((-EDGE_BETA * step) * step)

    cut_row = {
        ITERS - 1: jnp.where(gy == 0, 0.0, 1.0),
        ITERS + rows - 1: jnp.where(gy == last_gy, 0.0, 1.0),
    }
    for i in sorted(set(span["w_raw"]) | set(span["d_raw"])):
        here = smooth.row(i)
        if i in span["w_raw"]:
            after = smooth.row(i + 1)
            for t, p in every:
                value = weight(after(p, t) - here(p, t))
                w_raw.put(i, p, t, cut_row[i] * value if i in cut_row else value)
        if i in span["d_raw"]:
            beyond = shifted(here, 1)
            for t, p in every:
                if p == 0:
                    d_raw.put(i, p, t, weight(here(1, t) - here(0, t)))
                else:
                    d_raw.put(i, p, t, not_last * weight(next_sub(here(0, t)) - here(1, t)))
                value = weight(beyond(p, t) - here(p, t))
                c_raw.put(i, p, t, cut_tile[t] * value if t in cut_tile else value)

    for i in span["scale"]:
        dep, col, down, up = d_raw.row(i), c_raw.row(i), w_raw.row(i), w_raw.row(i - 1)
        col_back = shifted(col, -1)
        seeded = [mark.row(i) for mark in marks]
        for t, p in every:
            back = prev_sub(dep(1, t)) if p == 0 else dep(0, t)
            deg = dep(p, t) + back + down(p, t) + up(p, t) + col(p, t) + col_back(p, t)
            free = seeded[0](p, t) + seeded[1](p, t) == 0.0
            scale.put(i, p, t, jnp.where(free, lax.rsqrt(deg), 0.0))

    def neighbour_sum(v, field, i, dep, col, down, up):
        above, below = field.row(i - 1), field.row(i + 1)
        beyond = shifted(v, 1)
        pushed = shifted(lambda p, t: col(p, t) * v(p, t), -1)

        def total(p, t):
            if p == 0:
                depth = dep(0, t) * v(1, t) + prev_sub(dep(1, t) * v(1, t))
            else:
                depth = dep(1, t) * next_sub(v(0, t)) + dep(0, t) * v(0, t)
            return (depth + (col(p, t) * beyond(p, t) + pushed(p, t))) + (
                down(p, t) * below(p, t) + up(p, t) * above(p, t)
            )

        return once(total)

    for i in span["y", 0]:
        edges = d_raw.row(i), c_raw.row(i), w_raw.row(i), w_raw.row(i - 1)
        s = scale.row(i)
        totals = [neighbour_sum(mark.row(i), mark, i, *edges) for mark in marks]
        for t, p in every:
            for f in range(FIELDS):
                y[0][f].put(i, p, t, s(p, t) * totals[f](p, t))

    for i in sorted(set(span["w_row"]) | set(span["w_dep"])):
        s = scale.row(i)
        if i in span["w_row"]:
            after, down = scale.row(i + 1), w_raw.row(i)
            for t, p in every:
                w_row.put(i, p, t, down(p, t) * s(p, t) * after(p, t))
        if i in span["w_dep"]:
            dep, col = d_raw.row(i), c_raw.row(i)
            beyond = shifted(s, 1)
            for t, p in every:
                other = s(1, t) if p == 0 else next_sub(s(0, t))
                w_dep.put(i, p, t, dep(p, t) * s(p, t) * other)
                w_col.put(i, p, t, col(p, t) * s(p, t) * beyond(p, t))

    sums = [[None] * MOMENTS for _ in range(FIELDS)]

    def add_products(f, k, a, b):
        total = None
        for t, p in inner:
            part = a(p, t) * b(p, t)
            total = part if total is None else total + part
        sums[f][k] = total if sums[f][k] is None else sums[f][k] + total

    def keep_basis(level, i, values):
        s = scale.row(i)
        for t, p in inner:
            for f in range(FIELDS):
                lanes = slice(t * LANES, (t + 1) * LANES)
                basis[level, f, i - ITERS - basis_first, p, :, lanes] = s(p, t) * values[f](p, t)

    own = range(ITERS, ITERS + rows)
    for i in span["y", 0]:
        if i in own:
            values = [y[0][f].row(i) for f in range(FIELDS)]
            keep_basis(0, i, values)
            for f in range(FIELDS):
                add_products(f, 0, values[f], values[f])
    for level in range(1, ITERS):
        for i in span["y", level]:
            edges = w_dep.row(i), w_col.row(i), w_row.row(i), w_row.row(i - 1)
            olds = [y[level - 1][f].row(i) for f in range(FIELDS)]
            news = [neighbour_sum(olds[f], y[level - 1][f], i, *edges) for f in range(FIELDS)]
            for t, p in every:
                for f in range(FIELDS):
                    y[level][f].put(i, p, t, news[f](p, t))
            if i in own:
                keep_basis(level, i, news)
                for f in range(FIELDS):
                    add_products(f, 2 * level - 1, olds[f], news[f])
                    add_products(f, 2 * level, news[f], news[f])
    for i in span["edge"]:
        dep, col, row = w_dep.row(i), w_col.row(i), w_row.row(i)
        for f in range(FIELDS):
            v, below = y[ITERS - 1][f].row(i), y[ITERS - 1][f].row(i + 1)
            beyond = shifted(v, 1)

            def forward(p, t, v=v, below=below, beyond=beyond):
                lower = v(1, t) if p == 0 else next_sub(v(0, t))
                return dep(p, t) * lower + col(p, t) * beyond(p, t) + row(p, t) * below(p, t)

            add_products(f, MOMENTS - 1, once(forward), v)
    for f in range(FIELDS):
        for k in range(MOMENTS):
            partial[f, k] = sums[f][k]


def halo_tile(lane, before, before_at, after, after_at):
    after_tile = pltpu.roll(after, (LANES - after_at) % LANES, 1) if after_at else after
    shift = (LANES - 8 - before_at) % LANES
    before_tile = pltpu.roll(before, shift, 1) if shift else before
    return jnp.where(lane < 8, after_tile, jnp.where(lane >= LANES - 8, before_tile, 0.0))


def tiles_of(slab, halo):
    cols = slab.shape[-1]
    return [slab[:, at : at + LANES] for at in range(0, cols, LANES)] + [halo]


def corner_tile(lane, ref, kind, parity, row):
    tile = ref[kind, parity]
    place = (8 * row) % (LANES // 2)
    return halo_tile(lane, tile, LANES // 2 + place, tile, place)


STATE = ("image", "mark", *WEIGHTS, *(("y", level) for level in range(ITERS)))


def make_stores(rows, *parts):
    stores = {}

    def pieces(name):
        return [(extents(rows, part)[name], refs[STATE.index(name)]) for part, refs in parts]

    for name in ("image", *WEIGHTS):
        stores[name] = Rows(pieces(name))
    for f in range(FIELDS):
        stores["mark", f] = Rows(pieces("mark"), (f,))
        for level in range(ITERS):
            stores["y", level, f] = Rows(pieces(("y", level)), (f,))
    return stores


def middle_kernel(rows, half, own, label, from_left, from_right, *refs):
    state, (basis, partial) = refs[: len(STATE)], refs[len(STATE) :]

    def fetch(source, kind, before):
        def parts(i, p, lane):
            row = i - before
            halo = halo_tile(lane, from_left[kind, p], 8 * row, from_right[kind, p], 8 * row)
            return tiles_of(source.at[row, p], halo)

        return parts

    images, labels = fetch(own, 0, IMG_BEFORE), fetch(label, 1, SEED_BEFORE)
    stores = make_stores(rows, (MIDDLE, state))
    sweep(rows, half, MIDDLE, images, labels, stores, basis, partial)


def head_kernel(rows, half, above, corner_above, *refs):
    count = len(STATE)
    middle, (basis, partial), state = refs[:count], refs[count : count + 2], refs[count + 2 :]

    def fetch(kind, before, first):
        def parts(i, p, lane):
            halo = corner_tile(lane, corner_above, kind, p, rows + i - before)
            return tiles_of(above.at[first + i, p], halo)

        return parts

    images, labels = fetch(0, IMG_BEFORE, 0), fetch(1, SEED_BEFORE, IMG_BEFORE)
    stores = make_stores(rows, (HEAD, state), (MIDDLE, middle))
    sweep(rows, half, HEAD, images, labels, stores, basis, partial)


def tail_kernel(rows, half, below, corner_below, *refs):
    count = len(STATE)
    middle, refs = refs[:count], refs[count:]
    (others, (basis, stats), partial), state = (refs[:2], refs[2:4], refs[4]), refs[5:]

    def fetch(kind, before, first):
        def parts(i, p, lane):
            row = i - before - rows
            halo = corner_tile(lane, corner_below, kind, p, row)
            return tiles_of(below.at[first + row, p], halo)

        return parts

    images, labels = fetch(0, IMG_BEFORE, 0), fetch(1, SEED_BEFORE, IMG_AFTER)
    stores = make_stores(rows, (TAIL, state), (MIDDLE, middle))
    sweep(rows, half, TAIL, images, labels, stores, basis, partial)
    one_lane = lax.broadcasted_iota(jnp.int32, (1, LANES), 1)
    packed = jnp.zeros((1, LANES), jnp.float32)
    for f in range(FIELDS):
        for k in range(MOMENTS):
            whole = partial[f, k] + others[0][f, k] + others[1][f, k]
            whole = 2.0 * whole if k == MOMENTS - 1 else whole
            value = jnp.sum(jnp.sum(whole, axis=0, keepdims=True), axis=1, keepdims=True)
            packed = jnp.where(one_lane == f * MOMENTS + k, value, packed)
    stats[...] = packed


def combine(a, b):
    out = [None] * (len(a) + len(b) - 1)
    for i, x in enumerate(a):
        for j, z in enumerate(b):
            out[i + j] = x * z if out[i + j] is None else out[i + j] + x * z
    return out


def weighted(coefs, values):
    total = coefs[0] * values[0]
    for c, v in zip(coefs[1:], values[1:]):
        total = total + c * v
    return total


def krylov_coefs(m):
    gaps = [m[k] - m[k + 1] for k in range(MOMENTS - 1)]
    one = jnp.ones_like(m[0])
    zero = jnp.zeros_like(m[0])
    resid, direct, result = [one], [one], [zero] * ITERS
    rz = m[0]
    for k in range(ITERS):
        curve = weighted(combine(direct, direct), gaps)
        alpha = jnp.where(curve > 0.0, rz / curve, 0.0)
        result = [
            result[i] + alpha * direct[i] if i < len(direct) else result[i] for i in range(ITERS)
        ]
        if k + 1 == ITERS:
            break
        image = [
            (direct[i] if i < len(direct) else zero) - (direct[i - 1] if i > 0 else zero)
            for i in range(len(direct) + 1)
        ]
        resid = [(resid[i] if i < len(resid) else zero) - alpha * image[i] for i in range(len(image))]
        rz_next = weighted(combine(resid, resid), m)
        ratio = jnp.where(rz > 0.0, rz_next / rz, 0.0)
        direct = [
            resid[i] + ratio * direct[i] if i < len(direct) else resid[i] for i in range(len(resid))
        ]
        rz = rz_next
    return result


def finish_kernel(rows, half, gathered, middle, head, tail, label, out_hbm, out, out_sem):
    core_tiles = out.shape[1]
    total = jnp.sum(gathered[...], axis=0, keepdims=True)
    one_lane = lax.broadcasted_iota(jnp.int32, (1, LANES), 1)
    coefs = []
    for f in range(FIELDS):
        moments = []
        for k in range(MOMENTS):
            pick = jnp.where(one_lane == f * MOMENTS + k, total, 0.0)
            value = jnp.sum(pick, axis=1, keepdims=True)
            moments.append(jnp.broadcast_to(value, (half, LANES)))
        coefs.append(krylov_coefs(moments))
    depth_rows = 2 * half * rows
    copies = []
    for f in range(FIELDS):
        for t in range(core_tiles):
            at = slice(t * LANES, (t + 1) * LANES)
            for row in range(rows):
                for parity in range(2):
                    parts = []
                    for k in range(ITERS):
                        for part, basis in enumerate((middle, head, tail)):
                            if row + ITERS in extents(rows, part)["y", k]:
                                place = row - basis_span(rows, part).start
                                parts.append(basis[k, f, place, parity, :, at])
                    x = weighted(coefs[f], parts)
                    hit = label[row, parity, :, at] == f + 1.0
                    index = pl.ds(row + rows * parity, half, 2 * rows)
                    out[f, t, index, :] = x + hit.astype(jnp.float32)
            copy = pltpu.make_async_copy(
                out.at[f, t],
                out_hbm.at[pl.ds(f * depth_rows, depth_rows), pl.ds(t * LANES, LANES)],
                out_sem.at[f, t],
            )
            copy.start()
            copies.append(copy)
    for copy in copies:
        copy.wait()


def vmem(count):
    return [pl.BlockSpec(memory_space=pltpu.VMEM)] * count


def hbm(count):
    return [pl.BlockSpec(memory_space=pltpu.HBM)] * count


def on_device(image, seeds):
    depth, rows, cols = image.shape
    half = depth // 2
    wide = cols + LANES
    core_tiles = cols // LANES
    f32 = jnp.float32

    def call(kernel, name, shapes, raw, operands, scratch=(), raw_out=False, mib=16, cost=None):
        return pl.pallas_call(
            lambda *refs: kernel(rows, half, *refs),
            out_shape=[jax.ShapeDtypeStruct(shape, f32) for shape in shapes],
            in_specs=hbm(len(raw)) + vmem(len(operands)),
            out_specs=hbm(len(shapes)) if raw_out else vmem(len(shapes)),
            scratch_shapes=list(scratch),
            compiler_params=pltpu.CompilerParams(vmem_limit_bytes=mib * 1024 * 1024),
            cost_estimate=cost,
            name=name,
        )(*raw, *operands)

    def forward(x, axis):
        return lax.ppermute(x, axis, [(i, i + 1) for i in range(lax.axis_size(axis) - 1)])

    def backward(x, axis):
        return lax.ppermute(x, axis, [(i + 1, i) for i in range(lax.axis_size(axis) - 1)])

    def staged(dtype):
        return pltpu.VMEM((core_tiles, depth * rows, LANES), dtype)

    slabs = (rows, 2, half, cols)
    up, down, own, label = call(
        rows_kernel,
        "own_rows",
        [(UP,) + slabs[1:], (DOWN,) + slabs[1:], slabs, slabs],
        tuple(
            pltpu.with_memory_space_constraint(v.reshape(depth * rows, cols), pltpu.HBM)
            for v in (image, seeds)
        ),
        (),
        [staged(f32), staged(jnp.int32)] + [pltpu.SemaphoreType.DMA((core_tiles,))] * 2,
    )
    above = forward(up, "gy")
    below = backward(down, "gy")
    side = (2, 2, half, LANES)
    even = lax.rem(lax.axis_index("gz"), 2) == 0

    def swap_columns(own, label):
        pair, cross = call(cols_kernel, "own_columns", [side, side], (), (own, label))
        count = lax.axis_size("gz")
        within = [(i, i ^ 1) for i in range(count) if i ^ 1 < count]
        between = [(i, i + 1) for i in range(1, count - 1, 2)]
        pair = lax.ppermute(pair, "gz", within)
        cross = lax.ppermute(cross, "gz", between + [(j, i) for i, j in between])
        left, right = jnp.where(even, cross, pair), jnp.where(even, pair, cross)
        mid = LANES // 2
        corner_up = jnp.concatenate([right[..., mid:], left[..., mid:]], axis=-1)
        corner_down = jnp.concatenate([right[..., :mid], left[..., :mid]], axis=-1)
        return pair, cross, corner_up, corner_down

    def exchange_columns(own, label):
        return swap_columns(own, label)

    pair, cross, corner_up, corner_down = exchange_columns(own, label)
    from_left, from_right = jnp.where(even, cross, pair), jnp.where(even, pair, cross)
    corner_above = forward(corner_up, "gy")
    corner_below = backward(corner_down, "gy")

    def state_shapes(part):
        shapes = []
        for name in STATE:
            lead = () if name == "image" or name in WEIGHTS else (FIELDS,)
            shapes.append(lead + (len(extents(rows, part)[name]), 2, half, wide))
        return shapes

    def basis_shape(part):
        return (ITERS, FIELDS, len(basis_span(rows, part))) + slabs[1:]

    def scratch(part):
        return [pltpu.VMEM(shape, f32) for shape in state_shapes(part)]

    sums = (FIELDS, MOMENTS, half, LANES)
    *state, basis_middle, sums_middle = call(
        middle_kernel,
        "middle",
        state_shapes(MIDDLE) + [basis_shape(MIDDLE), sums],
        (),
        (own, label, from_left, from_right),
        cost=pl.CostEstimate(flops=0, bytes_accessed=MIDDLE_COST << 20, transcendentals=0),
    )
    basis_head, sums_head = call(
        head_kernel,
        "head",
        [basis_shape(HEAD), sums],
        (),
        (above, corner_above, *state),
        scratch(HEAD),
        cost=pl.CostEstimate(flops=0, bytes_accessed=8 << 20, transcendentals=0),
    )
    basis_tail, stats = call(
        tail_kernel,
        "tail",
        [basis_shape(TAIL), (1, LANES)],
        (),
        (below, corner_below, *state, sums_middle, sums_head),
        [pltpu.VMEM(sums, f32)] + scratch(TAIL),
    )
    devices = lax.axis_size("gy") * lax.axis_size("gz")
    spread = jnp.broadcast_to(stats[None], (devices, 1, LANES))
    gathered = lax.all_to_all(spread, ("gy", "gz"), 0, 0).reshape(devices, LANES)
    (out,) = call(
        finish_kernel,
        "finish",
        [(FIELDS * depth * rows, cols)],
        (),
        (gathered, basis_middle, basis_head, basis_tail, label),
        [
            pltpu.VMEM((FIELDS, core_tiles, depth * rows, LANES), f32),
            pltpu.SemaphoreType.DMA((FIELDS, core_tiles)),
        ],
        raw_out=True,
    )
    return out.reshape(FIELDS, depth, rows, cols)


def solution(mesh):
    return jax.shard_map(
        on_device,
        mesh=mesh,
        in_specs=(P(None, "gy", "gz"), P(None, "gy", "gz")),
        out_specs=P(None, None, "gy", "gz"),
        check_vma=False,
    )
```

```python
import math

import jax
import jax.numpy as jnp
from jax import lax
from jax.experimental import pallas as pl
from jax.experimental.pallas import tpu as pltpu
from jax.sharding import PartitionSpec as P

ITERS = 4
FIELDS = 2
EDGE_BETA = 60.0
EDGE_FLOOR = 0.05
LANES = 128

IMG_BEFORE, IMG_AFTER = ITERS + 2, ITERS + 3
SEED_BEFORE, SEED_AFTER = ITERS, ITERS + 1
UP = IMG_BEFORE + SEED_BEFORE
DOWN = IMG_AFTER + SEED_AFTER
MOMENTS = 2 * ITERS
MIDDLE_COST = 10


def gauss_taps():
    raw = [math.exp(-0.5 * k * k) for k in range(-2, 3)]
    total = sum(raw)
    return [value / total for value in raw]


def rows_kernel(rows, half, image_hbm, seeds_hbm, up, down, own, label, image, seeds, image_sem, seeds_sem):
    sources = ((image_hbm, image, image_sem), (seeds_hbm, seeds, seeds_sem))
    copies = [
        [
            pltpu.make_async_copy(source.at[:, pl.ds(t * LANES, LANES)], staged.at[t], sems.at[t])
            for source, staged, sems in sources
        ]
        for t in range(image.shape[0])
    ]
    for pair in copies:
        for copy in pair:
            copy.start()
    for t, pair in enumerate(copies):
        at = slice(t * LANES, (t + 1) * LANES)
        for copy in pair:
            copy.wait()
        for row in range(rows):
            for parity in range(2):
                index = pl.ds(row + rows * parity, half, 2 * rows)
                grey = image[t, index, :]
                seed = seeds[t, index, :].astype(jnp.float32)
                own[row, parity, :, at] = grey
                label[row, parity, :, at] = seed
                if row >= rows - IMG_BEFORE:
                    up[row - (rows - IMG_BEFORE), parity, :, at] = grey
                if row >= rows - SEED_BEFORE:
                    up[IMG_BEFORE + row - (rows - SEED_BEFORE), parity, :, at] = seed
                if row < IMG_AFTER:
                    down[row, parity, :, at] = grey
                if row < SEED_AFTER:
                    down[IMG_AFTER + row, parity, :, at] = seed


def cols_kernel(rows, half, own, label, pair, cross):
    even = lax.rem(lax.axis_index("gz"), 2) == 0
    cols = own.shape[3]
    lane = lax.broadcasted_iota(jnp.int32, (half, LANES), 1)
    for kind, source in enumerate((own, label)):
        for parity in range(2):
            head = jnp.zeros((half, LANES), jnp.float32)
            tail = jnp.zeros((half, LANES), jnp.float32)
            for row in range(rows):
                first = source[row, parity, :, 0:LANES]
                last = source[row, parity, :, cols - LANES : cols]
                here = (lane >= 8 * row) & (lane < 8 * row + 8)
                shift = (8 * row) % LANES
                head = jnp.where(here, pltpu.roll(first, shift, 1) if shift else first, head)
                shift = (8 * row + 8) % LANES
                tail = jnp.where(here, pltpu.roll(last, shift, 1) if shift else last, tail)
            pair[kind, parity] = jnp.where(even, tail, head)
            cross[kind, parity] = jnp.where(even, head, tail)


def once(get):
    known = {}

    def value(parity, t):
        if (parity, t) not in known:
            known[parity, t] = get(parity, t)
        return known[parity, t]

    return value


class Rows:
    def __init__(self, pieces, lead=()):
        self.pieces, self.lead = pieces, lead

    def place(self, start, i, parity, t):
        lanes = slice(t * LANES, (t + 1) * LANES)
        return (*self.lead, i - start, parity, slice(None), lanes)

    def row(self, i):
        for span, ref in self.pieces:
            if i in span:
                return once(lambda parity, t: ref[self.place(span.start, i, parity, t)])
        raise IndexError(i)

    def put(self, i, parity, t, value):
        span, ref = self.pieces[0]
        if i not in span:
            raise IndexError(i)
        ref[self.place(span.start, i, parity, t)] = value


MIDDLE, HEAD, TAIL = range(3)
WEIGHTS = ("smooth", "w_raw", "d_raw", "c_raw", "scale", "w_row", "w_dep", "w_col")


def extents(rows, part):
    low = IMG_BEFORE
    table = {
        "image": (0, low, rows + IMG_BEFORE, rows + IMG_BEFORE + IMG_AFTER),
        "mark": (0, SEED_BEFORE, rows + SEED_BEFORE, rows + SEED_BEFORE + SEED_AFTER),
        "smooth": (0, low, rows + 2, rows + 2 * ITERS + 1),
        "w_raw": (0, low, rows + 1, rows + 2 * ITERS),
        "d_raw": (1, low, rows + 2, rows + 2 * ITERS),
        "c_raw": (1, low, rows + 2, rows + 2 * ITERS),
        "scale": (1, low + 1, rows + 1, rows + 2 * ITERS),
        "w_row": (1, low + 1, rows, rows + 2 * ITERS - 1),
        "w_dep": (2, low + 1, rows + 1, rows + 2 * ITERS - 1),
        "w_col": (2, low + 1, rows + 1, rows + 2 * ITERS - 1),
        "edge": (ITERS, low + ITERS, rows + 1 - ITERS, rows + ITERS),
    }
    for level in range(ITERS):
        table["y", level] = (1 + level, low + 1 + level, rows + 1 - level, rows + 2 * ITERS - level)
    return {
        name: (range(low, high), range(first, low), range(high, stop))[part]
        for name, (first, low, high, stop) in table.items()
    }


def basis_span(rows, part):
    spans = [extents(rows, part)["y", level] for level in range(ITERS)]
    first = max(min(span.start for span in spans), ITERS)
    return range(first - ITERS, min(max(span.stop for span in spans), rows + ITERS) - ITERS)


def sweep(rows, half, part, fetch_image, fetch_seeds, stores, basis, partial):
    span = extents(rows, part)
    basis_first = basis_span(rows, part).start
    tiles = stores["smooth"].pieces[0][1].shape[-1] // LANES
    core_tiles = tiles - 1
    gy, gz = lax.axis_index("gy"), lax.axis_index("gz")
    last_gy, last_gz = lax.axis_size("gy") - 1, lax.axis_size("gz") - 1
    t0, t1, t2 = gauss_taps()[:3]
    sharp = math.sqrt(EDGE_BETA / math.log(2.0))
    lane = lax.broadcasted_iota(jnp.int32, (half, LANES), 1)
    sub = lax.broadcasted_iota(jnp.int32, (half, LANES), 0)
    not_first = (sub > 0).astype(jnp.float32)
    not_last = (sub < half - 1).astype(jnp.float32)
    every = [(t, p) for t in range(tiles) for p in range(2)]
    inner = [(t, p) for t in range(core_tiles) for p in range(2)]

    def shifted(get, by):
        turned = once(lambda parity, t: pltpu.roll(get(parity, t), -by % LANES, 1))
        if by > 0:
            return once(
                lambda parity, t: jnp.where(
                    lane < LANES - by, turned(parity, t), turned(parity, (t + 1) % tiles)
                )
            )
        return once(
            lambda parity, t: jnp.where(lane >= -by, turned(parity, t), turned(parity, (t - 1) % tiles))
        )

    def next_sub(v):
        return pltpu.roll(v, half - 1, 0)

    def prev_sub(v):
        return pltpu.roll(v, 1, 0)

    image, smooth, scale = stores["image"], stores["smooth"], stores["scale"]
    w_raw, d_raw, c_raw = stores["w_raw"], stores["d_raw"], stores["c_raw"]
    w_row, w_dep, w_col = stores["w_row"], stores["w_dep"], stores["w_col"]
    marks = [stores["mark", f] for f in range(FIELDS)]
    y = [[stores["y", level, f] for f in range(FIELDS)] for level in range(ITERS)]

    for i in span["image"]:
        for p in range(2):
            for t, part in enumerate(fetch_image(i, p, lane)):
                image.put(i, p, t, part)
    for i in span["mark"]:
        for p in range(2):
            for t, part in enumerate(fetch_seeds(i, p, lane)):
                for f in range(FIELDS):
                    marks[f].put(i, p, t, (part == f + 1.0).astype(jnp.float32))

    for i in span["smooth"]:
        x = [image.row(i + k) for k in range(5)]
        flat = once(
            lambda p, t, x=x: t0 * (x[0](p, t) + x[4](p, t))
            + t1 * (x[1](p, t) + x[3](p, t))
            + t2 * x[2](p, t)
        )
        later = once(lambda p, t, flat=flat: not_last * next_sub(flat(p, t)))
        sooner = once(lambda p, t, flat=flat: not_first * prev_sub(flat(p, t)))
        for t, p in every:
            near = flat(1, t) + sooner(1, t) if p == 0 else flat(0, t) + later(0, t)
            smooth.put(i, p, t, t0 * (later(p, t) + sooner(p, t)) + t1 * near + t2 * flat(p, t))
    for i in span["smooth"]:
        deep = smooth.row(i)
        near_next, near_prev = shifted(deep, 1), shifted(deep, -1)
        far_next, far_prev = shifted(deep, 2), shifted(deep, -2)
        fresh = [
            (
                p,
                t,
                sharp * t0 * (far_next(p, t) + far_prev(p, t))
                + sharp * t1 * (near_next(p, t) + near_prev(p, t))
                + sharp * t2 * deep(p, t),
            )
            for t, p in every
        ]
        for p, t, value in fresh:
            smooth.put(i, p, t, value)

    cut_tile = {
        core_tiles - 1: jnp.where((lane == LANES - 1) & (gz == last_gz), 0.0, 1.0),
        tiles - 1: jnp.where((lane == LANES - 1) & (gz == 0), 0.0, 1.0),
    }

    def weight(step):
        return EDGE_FLOOR + jnp.exp2(-(step * step))

    cut_row = {
        ITERS - 1: jnp.where(gy == 0, 0.0, 1.0),
        ITERS + rows - 1: jnp.where(gy == last_gy, 0.0, 1.0),
    }
    for i in sorted(set(span["w_raw"]) | set(span["d_raw"])):
        here = smooth.row(i)
        if i in span["w_raw"]:
            after = smooth.row(i + 1)
            for t, p in every:
                value = weight(after(p, t) - here(p, t))
                w_raw.put(i, p, t, cut_row[i] * value if i in cut_row else value)
        if i in span["d_raw"]:
            beyond = shifted(here, 1)
            for t, p in every:
                if p == 0:
                    d_raw.put(i, p, t, weight(here(1, t) - here(0, t)))
                else:
                    d_raw.put(i, p, t, not_last * weight(next_sub(here(0, t)) - here(1, t)))
                value = weight(beyond(p, t) - here(p, t))
                c_raw.put(i, p, t, cut_tile[t] * value if t in cut_tile else value)

    for i in span["scale"]:
        dep, col, down, up = d_raw.row(i), c_raw.row(i), w_raw.row(i), w_raw.row(i - 1)
        col_back = shifted(col, -1)
        seeded = [mark.row(i) for mark in marks]
        for t, p in every:
            back = prev_sub(dep(1, t)) if p == 0 else dep(0, t)
            deg = dep(p, t) + back + down(p, t) + up(p, t) + col(p, t) + col_back(p, t)
            free = seeded[0](p, t) + seeded[1](p, t) == 0.0
            scale.put(i, p, t, jnp.where(free, lax.rsqrt(deg), 0.0))

    def neighbour_sum(v, field, i, dep, col, down, up):
        above, below = field.row(i - 1), field.row(i + 1)
        beyond = shifted(v, 1)
        pushed = shifted(lambda p, t: col(p, t) * v(p, t), -1)

        def total(p, t):
            if p == 0:
                depth = dep(0, t) * v(1, t) + prev_sub(dep(1, t) * v(1, t))
            else:
                depth = dep(1, t) * next_sub(v(0, t)) + dep(0, t) * v(0, t)
            return (depth + (col(p, t) * beyond(p, t) + pushed(p, t))) + (
                down(p, t) * below(p, t) + up(p, t) * above(p, t)
            )

        return once(total)

    for i in span["y", 0]:
        edges = d_raw.row(i), c_raw.row(i), w_raw.row(i), w_raw.row(i - 1)
        s = scale.row(i)
        totals = [neighbour_sum(mark.row(i), mark, i, *edges) for mark in marks]
        for t, p in every:
            for f in range(FIELDS):
                y[0][f].put(i, p, t, s(p, t) * totals[f](p, t))

    for i in sorted(set(span["w_row"]) | set(span["w_dep"])):
        s = scale.row(i)
        if i in span["w_row"]:
            after, down = scale.row(i + 1), w_raw.row(i)
            for t, p in every:
                w_row.put(i, p, t, down(p, t) * s(p, t) * after(p, t))
        if i in span["w_dep"]:
            dep, col = d_raw.row(i), c_raw.row(i)
            beyond = shifted(s, 1)
            for t, p in every:
                other = s(1, t) if p == 0 else next_sub(s(0, t))
                w_dep.put(i, p, t, dep(p, t) * s(p, t) * other)
                w_col.put(i, p, t, col(p, t) * s(p, t) * beyond(p, t))

    sums = [[None] * MOMENTS for _ in range(FIELDS)]

    def add_products(f, k, a, b):
        total = None
        for t, p in inner:
            part = a(p, t) * b(p, t)
            total = part if total is None else total + part
        sums[f][k] = total if sums[f][k] is None else sums[f][k] + total

    def keep_basis(level, i, values):
        s = scale.row(i)
        for t, p in inner:
            for f in range(FIELDS):
                lanes = slice(t * LANES, (t + 1) * LANES)
                basis[level, f, i - ITERS - basis_first, p, :, lanes] = s(p, t) * values[f](p, t)

    own = range(ITERS, ITERS + rows)
    for i in span["y", 0]:
        if i in own:
            values = [y[0][f].row(i) for f in range(FIELDS)]
            keep_basis(0, i, values)
            for f in range(FIELDS):
                add_products(f, 0, values[f], values[f])
    for level in range(1, ITERS):
        for i in span["y", level]:
            edges = w_dep.row(i), w_col.row(i), w_row.row(i), w_row.row(i - 1)
            olds = [y[level - 1][f].row(i) for f in range(FIELDS)]
            news = [neighbour_sum(olds[f], y[level - 1][f], i, *edges) for f in range(FIELDS)]
            for t, p in every:
                for f in range(FIELDS):
                    y[level][f].put(i, p, t, news[f](p, t))
            if i in own:
                keep_basis(level, i, news)
                for f in range(FIELDS):
                    add_products(f, 2 * level - 1, olds[f], news[f])
                    add_products(f, 2 * level, news[f], news[f])
    for i in span["edge"]:
        dep, col, row = w_dep.row(i), w_col.row(i), w_row.row(i)
        for f in range(FIELDS):
            v, below = y[ITERS - 1][f].row(i), y[ITERS - 1][f].row(i + 1)
            beyond = shifted(v, 1)

            def forward(p, t, v=v, below=below, beyond=beyond):
                lower = v(1, t) if p == 0 else next_sub(v(0, t))
                return dep(p, t) * lower + col(p, t) * beyond(p, t) + row(p, t) * below(p, t)

            add_products(f, MOMENTS - 1, once(forward), v)
    for f in range(FIELDS):
        for k in range(MOMENTS):
            partial[f, k] = sums[f][k]


def halo_tile(lane, before, before_at, after, after_at):
    after_tile = pltpu.roll(after, (LANES - after_at) % LANES, 1) if after_at else after
    shift = (LANES - 8 - before_at) % LANES
    before_tile = pltpu.roll(before, shift, 1) if shift else before
    return jnp.where(lane < 8, after_tile, jnp.where(lane >= LANES - 8, before_tile, 0.0))


def tiles_of(slab, halo):
    cols = slab.shape[-1]
    return [slab[:, at : at + LANES] for at in range(0, cols, LANES)] + [halo]


def corner_tile(lane, ref, kind, parity, row):
    tile = ref[kind, parity]
    place = (8 * row) % (LANES // 2)
    return halo_tile(lane, tile, LANES // 2 + place, tile, place)


STATE = ("image", "mark", *WEIGHTS, *(("y", level) for level in range(ITERS)))


def make_stores(rows, *parts):
    stores = {}

    def pieces(name):
        return [(extents(rows, part)[name], refs[STATE.index(name)]) for part, refs in parts]

    for name in ("image", *WEIGHTS):
        stores[name] = Rows(pieces(name))
    for f in range(FIELDS):
        stores["mark", f] = Rows(pieces("mark"), (f,))
        for level in range(ITERS):
            stores["y", level, f] = Rows(pieces(("y", level)), (f,))
    return stores


def middle_kernel(rows, half, own, label, from_left, from_right, *refs):
    state, (basis, partial) = refs[: len(STATE)], refs[len(STATE) :]

    def fetch(source, kind, before):
        def parts(i, p, lane):
            row = i - before
            halo = halo_tile(lane, from_left[kind, p], 8 * row, from_right[kind, p], 8 * row)
            return tiles_of(source.at[row, p], halo)

        return parts

    images, labels = fetch(own, 0, IMG_BEFORE), fetch(label, 1, SEED_BEFORE)
    stores = make_stores(rows, (MIDDLE, state))
    sweep(rows, half, MIDDLE, images, labels, stores, basis, partial)


def head_kernel(rows, half, above, corner_above, *refs):
    count = len(STATE)
    middle, (basis, partial), state = refs[:count], refs[count : count + 2], refs[count + 2 :]

    def fetch(kind, before, first):
        def parts(i, p, lane):
            halo = corner_tile(lane, corner_above, kind, p, rows + i - before)
            return tiles_of(above.at[first + i, p], halo)

        return parts

    images, labels = fetch(0, IMG_BEFORE, 0), fetch(1, SEED_BEFORE, IMG_BEFORE)
    stores = make_stores(rows, (HEAD, state), (MIDDLE, middle))
    sweep(rows, half, HEAD, images, labels, stores, basis, partial)


def tail_kernel(rows, half, below, corner_below, *refs):
    count = len(STATE)
    middle, refs = refs[:count], refs[count:]
    (others, (basis, stats), partial), state = (refs[:2], refs[2:4], refs[4]), refs[5:]

    def fetch(kind, before, first):
        def parts(i, p, lane):
            row = i - before - rows
            halo = corner_tile(lane, corner_below, kind, p, row)
            return tiles_of(below.at[first + row, p], halo)

        return parts

    images, labels = fetch(0, IMG_BEFORE, 0), fetch(1, SEED_BEFORE, IMG_AFTER)
    stores = make_stores(rows, (TAIL, state), (MIDDLE, middle))
    sweep(rows, half, TAIL, images, labels, stores, basis, partial)
    one_lane = lax.broadcasted_iota(jnp.int32, (1, LANES), 1)
    packed = jnp.zeros((1, LANES), jnp.float32)
    for f in range(FIELDS):
        for k in range(MOMENTS):
            whole = partial[f, k] + others[0][f, k] + others[1][f, k]
            whole = 2.0 * whole if k == MOMENTS - 1 else whole
            value = jnp.sum(jnp.sum(whole, axis=0, keepdims=True), axis=1, keepdims=True)
            packed = jnp.where(one_lane == f * MOMENTS + k, value, packed)
    stats[...] = packed


def combine(a, b):
    out = [None] * (len(a) + len(b) - 1)
    for i, x in enumerate(a):
        for j, z in enumerate(b):
            out[i + j] = x * z if out[i + j] is None else out[i + j] + x * z
    return out


def weighted(coefs, values):
    total = coefs[0] * values[0]
    for c, v in zip(coefs[1:], values[1:]):
        total = total + c * v
    return total


def krylov_coefs(m):
    gaps = [m[k] - m[k + 1] for k in range(MOMENTS - 1)]
    one = jnp.ones_like(m[0])
    zero = jnp.zeros_like(m[0])
    resid, direct, result = [one], [one], [zero] * ITERS
    rz = m[0]
    for k in range(ITERS):
        curve = weighted(combine(direct, direct), gaps)
        alpha = jnp.where(curve > 0.0, rz / curve, 0.0)
        result = [
            result[i] + alpha * direct[i] if i < len(direct) else result[i] for i in range(ITERS)
        ]
        if k + 1 == ITERS:
            break
        image = [
            (direct[i] if i < len(direct) else zero) - (direct[i - 1] if i > 0 else zero)
            for i in range(len(direct) + 1)
        ]
        resid = [(resid[i] if i < len(resid) else zero) - alpha * image[i] for i in range(len(image))]
        rz_next = weighted(combine(resid, resid), m)
        ratio = jnp.where(rz > 0.0, rz_next / rz, 0.0)
        direct = [
            resid[i] + ratio * direct[i] if i < len(direct) else resid[i] for i in range(len(resid))
        ]
        rz = rz_next
    return result


def finish_kernel(rows, half, gathered, middle, head, tail, label, out_hbm, out, out_sem):
    core_tiles = out.shape[1]
    total = jnp.sum(gathered[...], axis=0, keepdims=True)
    one_lane = lax.broadcasted_iota(jnp.int32, (1, LANES), 1)
    coefs = []
    for f in range(FIELDS):
        moments = []
        for k in range(MOMENTS):
            pick = jnp.where(one_lane == f * MOMENTS + k, total, 0.0)
            value = jnp.sum(pick, axis=1, keepdims=True)
            moments.append(jnp.broadcast_to(value, (half, LANES)))
        coefs.append(krylov_coefs(moments))
    depth_rows = 2 * half * rows
    copies = []
    for f in range(FIELDS):
        for t in range(core_tiles):
            at = slice(t * LANES, (t + 1) * LANES)
            for row in range(rows):
                for parity in range(2):
                    parts = []
                    for k in range(ITERS):
                        for part, basis in enumerate((middle, head, tail)):
                            if row + ITERS in extents(rows, part)["y", k]:
                                place = row - basis_span(rows, part).start
                                parts.append(basis[k, f, place, parity, :, at])
                    x = weighted(coefs[f], parts)
                    hit = label[row, parity, :, at] == f + 1.0
                    index = pl.ds(row + rows * parity, half, 2 * rows)
                    out[f, t, index, :] = x + hit.astype(jnp.float32)
            copy = pltpu.make_async_copy(
                out.at[f, t],
                out_hbm.at[pl.ds(f * depth_rows, depth_rows), pl.ds(t * LANES, LANES)],
                out_sem.at[f, t],
            )
            copy.start()
            copies.append(copy)
    for copy in copies:
        copy.wait()


def vmem(count):
    return [pl.BlockSpec(memory_space=pltpu.VMEM)] * count


def hbm(count):
    return [pl.BlockSpec(memory_space=pltpu.HBM)] * count


def on_device(image, seeds):
    depth, rows, cols = image.shape
    half = depth // 2
    wide = cols + LANES
    core_tiles = cols // LANES
    f32 = jnp.float32

    def call(kernel, name, shapes, raw, operands, scratch=(), raw_out=False, mib=16, cost=None):
        return pl.pallas_call(
            lambda *refs: kernel(rows, half, *refs),
            out_shape=[jax.ShapeDtypeStruct(shape, f32) for shape in shapes],
            in_specs=hbm(len(raw)) + vmem(len(operands)),
            out_specs=hbm(len(shapes)) if raw_out else vmem(len(shapes)),
            scratch_shapes=list(scratch),
            compiler_params=pltpu.CompilerParams(vmem_limit_bytes=mib * 1024 * 1024),
            cost_estimate=cost,
            name=name,
        )(*raw, *operands)

    def forward(x, axis):
        return lax.ppermute(x, axis, [(i, i + 1) for i in range(lax.axis_size(axis) - 1)])

    def backward(x, axis):
        return lax.ppermute(x, axis, [(i + 1, i) for i in range(lax.axis_size(axis) - 1)])

    def staged(dtype):
        return pltpu.VMEM((core_tiles, depth * rows, LANES), dtype)

    slabs = (rows, 2, half, cols)
    up, down, own, label = call(
        rows_kernel,
        "own_rows",
        [(UP,) + slabs[1:], (DOWN,) + slabs[1:], slabs, slabs],
        tuple(
            pltpu.with_memory_space_constraint(v.reshape(depth * rows, cols), pltpu.HBM)
            for v in (image, seeds)
        ),
        (),
        [staged(f32), staged(jnp.int32)] + [pltpu.SemaphoreType.DMA((core_tiles,))] * 2,
    )
    above = forward(up, "gy")
    below = backward(down, "gy")
    side = (2, 2, half, LANES)
    even = lax.rem(lax.axis_index("gz"), 2) == 0

    def swap_columns(own, label):
        pair, cross = call(cols_kernel, "own_columns", [side, side], (), (own, label))
        count = lax.axis_size("gz")
        within = [(i, i ^ 1) for i in range(count) if i ^ 1 < count]
        between = [(i, i + 1) for i in range(1, count - 1, 2)]
        pair = lax.ppermute(pair, "gz", within)
        cross = lax.ppermute(cross, "gz", between + [(j, i) for i, j in between])
        left, right = jnp.where(even, cross, pair), jnp.where(even, pair, cross)
        mid = LANES // 2
        corner_up = jnp.concatenate([right[..., mid:], left[..., mid:]], axis=-1)
        corner_down = jnp.concatenate([right[..., :mid], left[..., :mid]], axis=-1)
        return pair, cross, corner_up, corner_down

    def exchange_columns(own, label):
        return swap_columns(own, label)

    pair, cross, corner_up, corner_down = exchange_columns(own, label)
    from_left, from_right = jnp.where(even, cross, pair), jnp.where(even, pair, cross)
    corner_above = forward(corner_up, "gy")
    corner_below = backward(corner_down, "gy")

    def state_shapes(part):
        shapes = []
        for name in STATE:
            lead = () if name == "image" or name in WEIGHTS else (FIELDS,)
            shapes.append(lead + (len(extents(rows, part)[name]), 2, half, wide))
        return shapes

    def basis_shape(part):
        return (ITERS, FIELDS, len(basis_span(rows, part))) + slabs[1:]

    def scratch(part):
        return [pltpu.VMEM(shape, f32) for shape in state_shapes(part)]

    sums = (FIELDS, MOMENTS, half, LANES)
    *state, basis_middle, sums_middle = call(
        middle_kernel,
        "middle",
        state_shapes(MIDDLE) + [basis_shape(MIDDLE), sums],
        (),
        (own, label, from_left, from_right),
        cost=pl.CostEstimate(flops=0, bytes_accessed=MIDDLE_COST << 20, transcendentals=0),
    )
    basis_head, sums_head = call(
        head_kernel,
        "head",
        [basis_shape(HEAD), sums],
        (),
        (above, corner_above, *state),
        scratch(HEAD),
        cost=pl.CostEstimate(flops=0, bytes_accessed=8 << 20, transcendentals=0),
    )
    basis_tail, stats = call(
        tail_kernel,
        "tail",
        [basis_shape(TAIL), (1, LANES)],
        (),
        (below, corner_below, *state, sums_middle, sums_head),
        [pltpu.VMEM(sums, f32)] + scratch(TAIL),
    )
    devices = lax.axis_size("gy") * lax.axis_size("gz")
    spread = jnp.broadcast_to(stats[None], (devices, 1, LANES))
    gathered = lax.all_to_all(spread, ("gy", "gz"), 0, 0).reshape(devices, LANES)
    (out,) = call(
        finish_kernel,
        "finish",
        [(FIELDS * depth * rows, cols)],
        (),
        (gathered, basis_middle, basis_head, basis_tail, label),
        [
            pltpu.VMEM((FIELDS, core_tiles, depth * rows, LANES), f32),
            pltpu.SemaphoreType.DMA((FIELDS, core_tiles)),
        ],
        raw_out=True,
    )
    return out.reshape(FIELDS, depth, rows, cols)


def solution(mesh):
    return jax.shard_map(
        on_device,
        mesh=mesh,
        in_specs=(P(None, "gy", "gz"), P(None, "gy", "gz")),
        out_specs=P(None, None, "gy", "gz"),
        check_vma=False,
    )
```
